512 devices in a mesh: prow: 32 (over x, y, core), pcol: 16 (over z).
Axes of the slice: x: 4, y: 4, z: 16, core: 2. Of those that a mesh axis runs over, the one named last changes fastest.
Arguments:
- slab: float32 [32768, 4096], P('prow', 'pcol'), may hold values from -6 to 6
- panel: float32 [32768, 256], P('prow', 'pcol'), may hold values from -0.1875 to 0.1875
- pivots: int32 [256], replicated, may hold values from 256 to 32767, as said below
Outputs:
- result: float32 [32768, 4096], P('prow', 'pcol')
The draws below stay inside these ranges and needn't reach their ends.
Inputs may be any that keep to these rules, and one draw needn't show every extreme that they name: `pivots`: 256 distinct rows, none among the first 256; at most 32 of them lie in the 1024 rows of one process row, and some process row holds exactly 32.
All inputs are finite; a program needn't handle non-finite values.
Results may differ from the reference program's by a relative error of at most 0.00005.
Values sent between devices are 32-bit elements; how exact they have to be, the bound alone decides.
A program may use at most 64 MiB of HBM per device.

```python
import jax
import jax.numpy as jnp
from jax import lax

NB = 256
ROWS = 1024
CAP = 32
M = 32768
NS = 4096
N_PROW = 32


def draw_pivots(key, part):
    total_slots = N_PROW * CAP
    heavy_row = jax.random.randint(jax.random.fold_in(key, 11), (), 0, N_PROW)
    slot_order = jax.random.permutation(jax.random.fold_in(key, 12), total_slots)
    slot_owner = slot_order // CAP
    slot_score = jnp.where(slot_owner == heavy_row, 0, total_slots) + jnp.arange(total_slots)
    ranked = slot_order[jnp.argsort(slot_score, stable=True)]
    chosen = jax.random.permutation(jax.random.fold_in(key, 13), ranked[:NB])
    owner_row = chosen // CAP
    slot_index = chosen % CAP
    stride = (ROWS - NB) // CAP
    jitter = jax.random.randint(jax.random.fold_in(key, 14), (NB,), 0, stride)
    return (owner_row * ROWS + NB + slot_index * stride + jitter).astype(jnp.int32)


def shard_levels(rng, shape, pieces, low, high):
    level = 1.0
    for dim, shards_of in pieces:
        steps = jax.random.uniform(jax.random.fold_in(jax.random.fold_in(rng, 6), dim), (shards_of,), jnp.float32, low / len(pieces), high / len(pieces))
        level = level * jnp.repeat(jnp.exp(steps), shape[dim] // shards_of).reshape((-1,) + (1,) * (len(shape) - 1 - dim))
    return level


def scatter_about(rng, extent, deviation, most, cuts=(), dtype=jnp.bfloat16):
    drawn = jax.random.normal(rng, extent, jnp.float32) * deviation
    if len(cuts) > 0:
        drawn = shard_levels(rng, extent, cuts, -0.22, 0.18) * drawn
    return jnp.clip(drawn, min=-most, max=most).astype(dtype)


def setup_inputs(seed: int = 0) -> dict:
    keys = jax.random.split(jax.random.key(seed), 4)
    return {
        "slab": scatter_about(keys[0], (M, NS), 1.0, 6.0, ((0, 32), (1, 16)), jnp.float32),
        "panel": scatter_about(keys[1], (M, NB), (4 * NB) ** -0.5, 0.1875, ((0, 32), (1, 16)), jnp.float32),
        "pivots": draw_pivots(jax.random.fold_in(keys[3], 71), 0),
    }


def reference(slab, panel, pivots):
    leading = slab[:NB]
    pivot_rows = slab[pivots]
    swapped = slab.at[pivots].set(leading)
    diag_block = panel[:NB]
    upper_rows = jax.scipy.linalg.solve_triangular(diag_block, pivot_rows, lower=True, unit_diagonal=True)
    update = jnp.dot(panel.astype(jnp.float32), upper_rows.astype(jnp.float32), precision=lax.Precision.HIGHEST, preferred_element_type=jnp.float32)
    result = swapped - update
    return result.at[:NB].set(upper_rows)
```

```python
import jax
import jax.numpy as jnp
from jax import lax
from jax.experimental import pallas as pl
from jax.experimental.pallas import tpu as pltpu
from jax.sharding import PartitionSpec as P

MESH = pl.DeviceIdType.MESH
F32 = jnp.float32
BF16 = jnp.bfloat16
NB = 256
ROWS = 1024
COLS = 256
NZ = 16
CHIPS = 16
HALF = 128
WIDTH = 16
STEPS = 8


def exchange_kernel(
    piv, slab, panel, pt, gathered, diag,
    rows, masked, from_sibling, landed, mine, lead_in, piece, piece_in, column,
    local_sem, ring_send, ring_recv, a_send, a_recv, b_send, b_recv, c_send, c_recv,
    lead_send, lead_recv, p_send, p_recv, rs_send, rs_recv, ag_send, ag_recv, sib_send, sib_recv,
):
    p = lax.axis_index("prow")
    z = lax.axis_index("pcol")
    chip = p // 2
    core = p % 2
    sibling = 2 * chip + 1 - core
    is_root = p == 0

    def near(o):
        return 2 * ((chip + o) % CHIPS) + core

    def above(o):
        return (z + o) % NZ

    barrier = pltpu.get_barrier_semaphore()

    def greet(device):
        pl.semaphore_signal(barrier, inc=1, device_id=device, device_id_type=MESH)

    def greet_planar(o, carry):
        greet((near(o), z))
        return carry

    def greet_column(o, carry):
        greet((p, above(o)))
        return carry

    lax.fori_loop(1, NZ, greet_column, 0)
    lax.fori_loop(1, CHIPS, greet_planar, 0)
    greet((sibling, z))

    def far(o):
        return (2 * o + 1, z)

    @pl.when(is_root)
    def _():
        def body(o, carry):
            greet(far(o))
            return carry
        lax.fori_loop(1, CHIPS, body, 0)

    @pl.when((core == 1) & (chip > 0))
    def _():
        greet((0, z))

    panel_copy = pltpu.make_async_copy(panel, pt.at[z], local_sem.at[0])
    slab_copy = pltpu.make_async_copy(slab, rows, local_sem.at[1])
    panel_copy.start()
    slab_copy.start()
    panel_copy.wait()
    for k in range(WIDTH):
        for h in range(2):
            piece[2 * k + h] = pt[z, k : k + 1, h * HALF : (h + 1) * HALF]
    slab_copy.wait()

    row_start = p * ROWS

    def pick(k, carry):
        local = piv[k] - row_start
        held = (local >= 0) & (local < ROWS)
        row = rows[pl.ds(jnp.clip(local, 0, ROWS - 1), 1), :]
        row = jnp.where(held, row, 0.0)
        masked[0, pl.ds(k, 1), :] = row[:, :HALF]
        masked[1, pl.ds(k, 1), :] = row[:, HALF:]
        return carry

    lax.fori_loop(0, NB, pick, 0, unroll=8)

    extra = jnp.where(is_root, 15, jnp.where((core == 1) & (chip > 0), 1, 0))
    pl.semaphore_wait(barrier, 31 + extra)

    def remote(src, dst, send, recv, device):
        return pltpu.make_async_remote_copy(
            src_ref=src, dst_ref=dst, send_sem=send, recv_sem=recv, device_id=device, device_id_type=MESH
        )

    def ring_copy(direction, step, half):
        block = (z - direction * step) % NZ
        part = pt.at[block, pl.ds(8 * half, 8)]
        d = (direction + 1) // 2
        return remote(
            part, part, ring_send.at[d, step, half], ring_recv.at[d, step, half], (p, (z + direction) % NZ)
        )

    def ring_uses(direction, step, half):
        if step < STEPS - 1:
            return True
        return step == STEPS - 1 and half == (0 if direction == 1 else 1)

    ring_legs = [(d, h) for h in range(2) for d in (1, -1)]

    def ring_step(step):
        for d, h in ring_legs:
            if step > 0 and ring_uses(d, step - 1, h):
                ring_copy(d, step - 1, h).wait_recv()
            if ring_uses(d, step, h):
                ring_copy(d, step, h).start()

    def a_copy(target):
        return remote(piece.at[target], piece_in.at[z], a_send.at[target], a_recv, (target, z))

    def lead_copy(target):
        t_chip, t_core = target // 2, target % 2
        src = rows.at[pl.ds(t_chip * 16, 16), pl.ds(pl.multiple_of(t_core * HALF, HALF), HALF)]
        return remote(src, lead_in, lead_send.at[target], lead_recv, (target, z))

    @pl.when(is_root)
    def _():
        def body(t, carry):
            a_copy(t).start()
            return carry
        lax.fori_loop(1, 2 * CHIPS, body, 0)
        piece_in[z] = piece[0]

    sib_p = remote(masked.at[1 - core], from_sibling, p_send, p_recv, (sibling, z))
    sib_p.start()

    ring_step(0)

    @pl.when(is_root)
    def _():
        def body(t, carry):
            lead_copy(t).start()
            return carry
        lax.fori_loop(1, 2 * CHIPS, body, 0)
        lead_in[...] = rows[0:16, 0:HALF]

    sib_p.wait_recv()
    masked[2] = masked[core] + from_sibling[...]

    def rs_copy(o):
        t_chip = (chip + o) % CHIPS
        return remote(
            masked.at[2, pl.ds(t_chip * 16, 16)], landed.at[o], rs_send.at[o], rs_recv.at[o], (near(o), z)
        )

    def loop(first, last, act):
        def body(o, carry):
            act(o)
            return carry
        lax.fori_loop(first, last, body, 0)

    loop(1, CHIPS, lambda o: rs_copy(o).start())

    ring_step(1)

    @pl.when(p > 0)
    def _():
        a_copy(p).wait_recv()

    def b_copy(o):
        return remote(piece_in.at[z], piece_in.at[z], b_send.at[o], b_recv.at[o], (p, above(o)))

    loop(1, NZ, lambda o: b_copy(o).start())

    ring_step(2)

    loop(1, CHIPS, lambda o: rs_copy(o).wait_recv())

    @pl.when(p > 0)
    def _():
        lead_copy(p).wait_recv()

    total = masked[2, pl.ds(chip * 16, 16)]
    for o in range(1, CHIPS):
        total = total + landed[o]
    mine[0] = total
    mine[1] = lead_in[...]
    gathered[core, chip] = mine[...]

    def ag_copy(o):
        return remote(mine, gathered.at[core, chip], ag_send.at[o], ag_recv.at[o], (near(o), z))

    loop(1, CHIPS, lambda o: ag_copy(o).start())

    ring_step(3)

    loop(1, NZ, lambda o: b_copy(o).wait_recv())
    for k in range(NZ):
        column[k : k + 1, :] = piece_in[k]
    diag[core, chip] = column[...]

    def c_copy(o):
        return remote(column, diag.at[core, chip], c_send.at[o], c_recv.at[o], (near(o), z))

    loop(1, CHIPS, lambda o: c_copy(o).start())

    ring_step(4)

    loop(1, CHIPS, lambda o: ag_copy(o).wait_recv())
    sib_g = remote(gathered.at[core], gathered.at[core], sib_send.at[0], sib_recv.at[0], (sibling, z))
    sib_g.start()

    ring_step(5)

    loop(1, CHIPS, lambda o: c_copy(o).wait_recv())
    sib_d = remote(diag.at[core], diag.at[core], sib_send.at[1], sib_recv.at[1], (sibling, z))
    sib_d.start()

    ring_step(6)
    ring_step(7)
    ring_step(8)

    sib_g.wait_recv()
    sib_d.wait_recv()

    sib_p.wait_send()
    sib_g.wait_send()
    sib_d.wait_send()
    loop(1, CHIPS, lambda o: rs_copy(o).wait_send())
    loop(1, CHIPS, lambda o: ag_copy(o).wait_send())
    loop(1, CHIPS, lambda o: c_copy(o).wait_send())
    loop(1, NZ, lambda o: b_copy(o).wait_send())
    for step in range(STEPS):
        for d, h in ring_legs:
            if ring_uses(d, step, h):
                ring_copy(d, step, h).wait_send()

    @pl.when(is_root)
    def _():
        def body(t, carry):
            a_copy(t).wait_send()
            lead_copy(t).wait_send()
            return carry
        lax.fori_loop(1, 2 * CHIPS, body, 0)


def exchange(slab, panel_t, pivots):
    dma = pltpu.SemaphoreType.DMA
    return pl.pallas_call(
        exchange_kernel,
        name="exchange",
        out_shape=(
            jax.ShapeDtypeStruct((NZ, WIDTH, ROWS), F32),
            jax.ShapeDtypeStruct((2, CHIPS, 2, 16, HALF), F32),
            jax.ShapeDtypeStruct((2, CHIPS, NZ, HALF), F32),
        ),
        in_specs=[
            pl.BlockSpec(memory_space=pltpu.SMEM),
            pl.BlockSpec(memory_space=pl.ANY),
            pl.BlockSpec(memory_space=pl.ANY),
        ],
        out_specs=(pl.BlockSpec(memory_space=pltpu.VMEM),) * 3,
        scratch_shapes=[
            pltpu.VMEM((ROWS, COLS), F32),
            pltpu.VMEM((3, NB, HALF), F32),
            pltpu.VMEM((NB, HALF), F32),
            pltpu.VMEM((CHIPS, 16, HALF), F32),
            pltpu.VMEM((2, 16, HALF), F32),
            pltpu.VMEM((16, HALF), F32),
            pltpu.VMEM((2 * CHIPS, 1, HALF), F32),
            pltpu.VMEM((NZ, 1, HALF), F32),
            pltpu.VMEM((NZ, HALF), F32),
            dma((2,)),
            dma((2, STEPS, 2)), dma((2, STEPS, 2)),
            dma((2 * CHIPS,)), dma,
            dma((NZ,)), dma((NZ,)),
            dma((CHIPS,)), dma((CHIPS,)),
            dma((2 * CHIPS,)), dma,
            dma, dma,
            dma((CHIPS,)), dma((CHIPS,)),
            dma((CHIPS,)), dma((CHIPS,)),
            dma((2,)), dma((2,)),
        ],
        compiler_params=pltpu.CompilerParams(
            collective_id=0, has_side_effects=True, vmem_limit_bytes=24 * 1024 * 1024
        ),
    )(pivots, slab, panel_t)


def split(a):
    high = a.astype(BF16)
    return high, (a - high.astype(F32)).astype(BF16)


def dot3(a, b, dims=(((1,), (0,)), ((), ()))):
    def one(x, y):
        return lax.dot_general(x, y, dims, preferred_element_type=F32)

    return one(a[0], b[0]) + (one(a[0], b[1]) + one(a[1], b[0]))


def invert(lower):
    row = lax.broadcasted_iota(jnp.int32, (NB, NB), 0)
    col = lax.broadcasted_iota(jnp.int32, (NB, NB), 1)
    base = 16
    blocks = NB // base
    on_diag = (row // base) == (col // base)
    packed = jnp.sum(jnp.where(on_diag, lower, 0.0).reshape(blocks, base, NB), axis=0)
    small_row = lax.broadcasted_iota(jnp.int32, (base, NB), 0)
    small_col = lax.broadcasted_iota(jnp.int32, (base, NB), 1)
    lane = lax.broadcasted_iota(jnp.int32, (base, HALF), 1)
    inverse = jnp.where(small_row == small_col % base, 1.0, 0.0)
    for k in range(base - 1):
        index = (lane // base) * base + k
        factor = jnp.concatenate(
            [jnp.take_along_axis(packed[:, h * HALF : (h + 1) * HALF], index, axis=1) for h in range(2)], axis=1
        )
        inverse = inverse - factor * inverse[k : k + 1, :]
    inverse = jnp.where(on_diag, jnp.concatenate([inverse] * blocks, axis=0), 0.0)
    size = base
    while size < NB:
        same = (row // (2 * size)) == (col // (2 * size))
        below = same & ((row // size) % 2 == 1) & ((col // size) % 2 == 0)
        corner = jnp.where(below, lower, 0.0)
        parts = split(inverse)
        inverse = inverse - dot3(parts, split(dot3(split(corner), parts)))
        size *= 2
    return inverse


def update_kernel(piv, slab, pt, gathered, diag, out, rows, leading, upper_t, result, load_sem, store_sem):
    p = lax.axis_index("prow")
    load = pltpu.make_async_copy(slab, rows.at[pl.ds(0, ROWS)], load_sem)
    load.start()

    for h in range(2):
        for z in range(NZ):
            upper_t[z * 16 : (z + 1) * 16, h * HALF : (h + 1) * HALF] = diag[h, pl.ds(z, 16, stride=NZ), :]
    row = lax.broadcasted_iota(jnp.int32, (NB, NB), 0)
    col = lax.broadcasted_iota(jnp.int32, (NB, NB), 1)
    lower = jnp.where(row > col, upper_t[...].T, 0.0)
    inverse = invert(lower)
    pivot_rows = jnp.concatenate([gathered[h, :, 0].reshape(NB, HALF) for h in range(2)], axis=1)
    upper = dot3(split(inverse), split(pivot_rows))
    upper_parts = split(upper)

    load.wait()

    def swap(k, carry):
        local = piv[k] - p * ROWS
        held = (local >= 0) & (local < ROWS)
        target = jnp.where(held, local, ROWS)
        rows[pl.ds(target, 1), :] = leading[pl.ds(k, 1), :]
        return carry

    for h in range(2):
        leading[:, h * HALF : (h + 1) * HALF] = gathered[h, :, 1].reshape(NB, HALF)
    lax.fori_loop(0, NB, swap, 0, unroll=8)

    chunk = 256
    for n in range(ROWS // chunk):
        block = pt[:, n * chunk : (n + 1) * chunk]
        product = dot3(split(block), upper_parts, (((0,), (0,)), ((), ())))
        value = rows[n * chunk : (n + 1) * chunk, :] - product
        if n == 0:
            value = jnp.where(p == 0, upper, value)
        result[n * chunk : (n + 1) * chunk, :] = value
        pltpu.make_async_copy(
            result.at[pl.ds(n * chunk, chunk)], out.at[pl.ds(n * chunk, chunk)], store_sem.at[n]
        ).start()
    for n in range(ROWS // chunk):
        pltpu.make_async_copy(
            result.at[pl.ds(n * chunk, chunk)], out.at[pl.ds(n * chunk, chunk)], store_sem.at[n]
        ).wait()


def finish(slab, pivots, pt, gathered, diag):
    vmem = pl.BlockSpec(memory_space=pltpu.VMEM)
    hbm = pl.BlockSpec(memory_space=pl.ANY)
    return pl.pallas_call(
        update_kernel,
        name="finish",
        out_shape=jax.ShapeDtypeStruct((ROWS, COLS), F32),
        in_specs=[pl.BlockSpec(memory_space=pltpu.SMEM), hbm, vmem, vmem, vmem],
        out_specs=hbm,
        scratch_shapes=[
            pltpu.VMEM((ROWS + 8, COLS), F32),
            pltpu.VMEM((NB, COLS), F32),
            pltpu.VMEM((NB, NB), F32),
            pltpu.VMEM((ROWS, COLS), F32),
            pltpu.SemaphoreType.DMA,
            pltpu.SemaphoreType.DMA((4,)),
        ],
        compiler_params=pltpu.CompilerParams(vmem_limit_bytes=32 * 1024 * 1024),
    )(pivots, slab, pt.reshape(NZ * WIDTH, ROWS), gathered, diag.reshape(2, NB, HALF))


def local(slab, panel, pivots):
    pt, gathered, diag = exchange(slab, panel.T, pivots)
    return finish(slab, pivots, pt, gathered, diag)


def solution(mesh):
    return jax.shard_map(
        local,
        mesh=mesh,
        in_specs=(P("prow", "pcol"), P("prow", "pcol"), P()),
        out_specs=P("prow", "pcol"),
        check_vma=False,
    )
```

```python
import jax
import jax.numpy as jnp
from jax import lax
from jax.experimental import pallas as pl
from jax.experimental.pallas import tpu as pltpu
from jax.sharding import PartitionSpec as P

MESH = pl.DeviceIdType.MESH
F32 = jnp.float32
BF16 = jnp.bfloat16
NB = 256
ROWS = 1024
COLS = 256
NZ = 16
CHIPS = 16
HALF = 128
WIDTH = 16
LAST = 8
JUMP = 3
REACH = 4


def exchange_kernel(
    pivots, slab, panel, pt, gathered, diag,
    piv, rows, masked, from_sibling, landed, mine, lead_in, piece, piece_in, column,
    local_sem, ring_send, ring_recv, a_send, a_recv, near_send, near_recv, far_send, far_recv, c_send, c_recv,
    lead_send, lead_recv, p_send, p_recv, rs_send, rs_recv, ag_send, ag_recv, sib_send, sib_recv,
):
    p = lax.axis_index("prow")
    z = lax.axis_index("pcol")
    chip = lax.div(p, 2)
    core = lax.rem(p, 2)
    sibling = 2 * chip + 1 - core
    is_root = p == 0
    outer = (core == 1) & (chip > 0)

    def loop(first, last, act):
        def body(o, carry):
            act(o)
            return carry
        lax.fori_loop(first, last, body, 0)

    def near(o):
        return 2 * lax.rem(chip + o, CHIPS) + core

    def above(o):
        return lax.rem(z + o + NZ, NZ)

    barrier = pltpu.get_barrier_semaphore()

    def greet(device):
        pl.semaphore_signal(barrier, inc=1, device_id=device, device_id_type=MESH)

    pivot_copy = pltpu.make_async_copy(pivots, piv, local_sem.at[2])
    panel_copy = pltpu.make_async_copy(panel, pt.at[z], local_sem.at[0])
    slab_copy = pltpu.make_async_copy(slab, rows, local_sem.at[1])
    pivot_copy.start()
    panel_copy.start()
    slab_copy.start()

    for o in range(1, REACH + 1):
        greet((p, above(o)))
        greet((p, above(-o)))
    loop(1, CHIPS, lambda o: greet((near(o), z)))
    greet((sibling, z))

    @pl.when(is_root)
    def _():
        loop(1, CHIPS, lambda o: greet((2 * o + 1, z)))

    @pl.when(outer)
    def _():
        greet((0, z))

    panel_copy.wait()
    for k in range(WIDTH):
        for h in range(2):
            piece[2 * k + h] = pt[z, k : k + 1, h * HALF : (h + 1) * HALF]
    pivot_copy.wait()
    slab_copy.wait()

    row_start = p * ROWS

    def pick(k, carry):
        local = piv[k] - row_start
        held = (local >= 0) & (local < ROWS)
        row = rows[pl.ds(jnp.clip(local, 0, ROWS - 1), 1), :]
        row = jnp.where(held, row, 0.0)
        masked[0, pl.ds(k, 1), :] = row[:, :HALF]
        masked[1, pl.ds(k, 1), :] = row[:, HALF:]
        return carry

    lax.fori_loop(0, NB, pick, 0, unroll=8)

    greeted = 2 * REACH + CHIPS
    pl.semaphore_wait(barrier, greeted + jnp.where(is_root, CHIPS - 1, jnp.where(outer, 1, 0)))

    def remote(src, dst, send, recv, device):
        return pltpu.make_async_remote_copy(
            src_ref=src, dst_ref=dst, send_sem=send, recv_sem=recv, device_id=device, device_id_type=MESH
        )

    def ring_copy(direction, place, half):
        jump = JUMP if place == JUMP else 1
        block = above(-direction * (place - jump))
        part = pt.at[block, pl.ds(8 * half, 8)]
        d = (direction + 1) // 2
        return remote(
            part, part, ring_send.at[d, place, half], ring_recv.at[d, place, half], (p, above(direction * jump))
        )

    def ring_uses(direction, place, half):
        return place < LAST or half == (0 if direction == 1 else 1)

    ring_legs = [(d, h) for h in range(2) for d in (1, -1)]

    def ring_first():
        for place in (JUMP, 1):
            for d, h in ring_legs:
                ring_copy(d, place, h).start()

    def ring_pass(place):
        for d, h in ring_legs:
            if ring_uses(d, place, h):
                ring_copy(d, place, h).wait_recv()
            if place + 1 != JUMP and place < LAST and ring_uses(d, place + 1, h):
                ring_copy(d, place + 1, h).start()

    def a_copy(target):
        return remote(piece.at[target], piece_in.at[z], a_send, a_recv, (target, z))

    def lead_copy(target):
        t_chip, t_core = lax.div(target, 2), lax.rem(target, 2)
        src = rows.at[pl.ds(t_chip * 16, 16), pl.ds(pl.multiple_of(t_core * HALF, HALF), HALF)]
        return remote(src, lead_in, lead_send.at[target], lead_recv, (target, z))

    def rs_copy(o):
        t_chip = lax.rem(chip + o, CHIPS)
        return remote(masked.at[2, pl.ds(t_chip * 16, 16)], landed.at[o], rs_send, rs_recv, (near(o), z))

    def ag_copy(o):
        return remote(mine, gathered.at[core, chip], ag_send, ag_recv, (near(o), z))

    def c_copy(o):
        return remote(column, diag.at[core, chip], c_send, c_recv, (near(o), z))

    def b_copy(source, to, send, recv):
        part = piece_in.at[above(source)]
        return remote(part, part, send, recv, (p, above(to)))

    sib_p = remote(masked.at[1 - core], from_sibling, p_send, p_recv, (sibling, z))
    sib_g = remote(gathered.at[core], gathered.at[core], sib_send.at[0], sib_recv.at[0], (sibling, z))
    sib_d = remote(diag.at[core], diag.at[core], sib_send.at[1], sib_recv.at[1], (sibling, z))
    here = (p, z)
    rs_all = remote(masked.at[2, pl.ds(0, 15 * 16)], landed.at[pl.ds(1, 15)], rs_send, rs_recv, here)
    ag_all = remote(gathered.at[core, pl.ds(0, 15)], gathered.at[core, pl.ds(0, 15)], ag_send, ag_recv, here)
    c_all = remote(diag.at[core, pl.ds(0, 15)], diag.at[core, pl.ds(0, 15)], c_send, c_recv, here)
    near_all = remote(piece_in.at[pl.ds(0, 8)], piece_in.at[pl.ds(0, 8)], near_send, near_recv, here)
    far_all = remote(piece_in.at[pl.ds(0, 7)], piece_in.at[pl.ds(0, 7)], far_send, far_recv, here)
    a_all = remote(piece.at[pl.ds(1, 31)], piece.at[pl.ds(1, 31)], a_send, a_recv, here)

    def a_start():
        @pl.when(is_root)
        def _():
            loop(1, 2 * CHIPS, lambda t: a_copy(t).start())
            piece_in[z] = piece[0]

    def lead_start():
        @pl.when(is_root)
        def _():
            loop(1, 2 * CHIPS, lambda t: lead_copy(t).start())
            lead_in[...] = rows[0:16, 0:HALF]

    def near_start():
        @pl.when(p > 0)
        def _():
            a_copy(p).wait_recv()
        for o in range(1, REACH + 1):
            b_copy(0, o, near_send, near_recv).start()
            b_copy(0, -o, near_send, near_recv).start()

    def far_start():
        near_all.wait_recv()
        for o in range(1, REACH + 1):
            b_copy(-o, REACH, far_send, far_recv).start()
            if o < REACH:
                b_copy(o, -REACH, far_send, far_recv).start()

    def c_start():
        far_all.wait_recv()
        for k in range(NZ):
            column[k : k + 1, :] = piece_in[k]
        diag[core, chip] = column[...]
        loop(1, CHIPS, lambda o: c_copy(o).start())

    def d_start():
        c_all.wait_recv()
        sib_d.start()

    def rs_start():
        sib_p.wait_recv()
        masked[2] = masked[core] + from_sibling[...]
        loop(1, CHIPS, lambda o: rs_copy(o).start())

    def ag_start():
        rs_all.wait_recv()
        @pl.when(p > 0)
        def _():
            lead_copy(p).wait_recv()
        total = masked[2, pl.ds(chip * 16, 16)]
        for o in range(1, CHIPS):
            total = total + landed[o]
        mine[0] = total
        mine[1] = lead_in[...]
        gathered[core, chip] = mine[...]
        loop(1, CHIPS, lambda o: ag_copy(o).start())

    def g_start():
        ag_all.wait_recv()
        sib_g.start()

    a_start()
    sib_p.start()
    ring_first()
    lead_start()
    rs_start()
    ring_pass(1)
    near_start()
    ring_pass(3)
    ag_start()
    far_start()
    ring_pass(4)
    g_start()
    ring_pass(5)
    c_start()
    ring_pass(6)
    d_start()
    ring_pass(7)
    ring_pass(8)
    ring_pass(2)
    sib_g.wait_recv()
    sib_d.wait_recv()

    for copy in (sib_p, sib_g, sib_d, rs_all, ag_all, c_all, near_all, far_all):
        copy.wait_send()
    for place in range(1, LAST + 1):
        for d, h in ring_legs:
            if ring_uses(d, place, h):
                ring_copy(d, place, h).wait_send()

    @pl.when(is_root)
    def _():
        a_all.wait_send()
        loop(1, 2 * CHIPS, lambda t: lead_copy(t).wait_send())


def exchange(slab, panel_t, pivots):
    dma = pltpu.SemaphoreType.DMA
    hbm = pl.BlockSpec(memory_space=pltpu.HBM)
    return pl.pallas_call(
        exchange_kernel,
        name="exchange",
        out_shape=(
            jax.ShapeDtypeStruct((NZ, WIDTH, ROWS), F32),
            jax.ShapeDtypeStruct((2, CHIPS, 2, 16, HALF), F32),
            jax.ShapeDtypeStruct((2, CHIPS, NZ, HALF), F32),
        ),
        in_specs=[hbm] * 3,
        out_specs=(pl.BlockSpec(memory_space=pltpu.VMEM),) * 3,
        scratch_shapes=[
            pltpu.SMEM((NB,), jnp.int32),
            pltpu.VMEM((ROWS, COLS), F32),
            pltpu.VMEM((3, NB, HALF), F32),
            pltpu.VMEM((NB, HALF), F32),
            pltpu.VMEM((CHIPS, 16, HALF), F32),
            pltpu.VMEM((2, 16, HALF), F32),
            pltpu.VMEM((16, HALF), F32),
            pltpu.VMEM((2 * CHIPS, 1, HALF), F32),
            pltpu.VMEM((NZ, 1, HALF), F32),
            pltpu.VMEM((NZ, HALF), F32),
            dma((3,)),
            dma((2, LAST + 1, 2)), dma((2, LAST + 1, 2)),
            dma, dma,
            dma, dma,
            dma, dma,
            dma, dma,
            dma((2 * CHIPS,)), dma,
            dma, dma,
            dma, dma,
            dma, dma,
            dma((2,)), dma((2,)),
        ],
        compiler_params=pltpu.CompilerParams(
            collective_id=0, has_side_effects=True, vmem_limit_bytes=24 * 1024 * 1024
        ),
    )(pivots, slab, panel_t)


def split(a):
    high = a.astype(BF16)
    return high, (a - high.astype(F32)).astype(BF16)


def dot3(a, b, dims=(((1,), (0,)), ((), ()))):
    def one(x, y):
        return lax.dot_general(x, y, dims, preferred_element_type=F32)

    return one(a[0], b[0]) + (one(a[0], b[1]) + one(a[1], b[0]))


def invert(lower):
    row = lax.broadcasted_iota(jnp.int32, (NB, NB), 0)
    col = lax.broadcasted_iota(jnp.int32, (NB, NB), 1)
    base = 16
    blocks = NB // base
    on_diag = (row // base) == (col // base)
    packed = jnp.sum(jnp.where(on_diag, lower, 0.0).reshape(blocks, base, NB), axis=0)
    small_row = lax.broadcasted_iota(jnp.int32, (base, NB), 0)
    small_col = lax.broadcasted_iota(jnp.int32, (base, NB), 1)
    lane = lax.broadcasted_iota(jnp.int32, (base, HALF), 1)
    inverse = jnp.where(small_row == small_col % base, 1.0, 0.0)
    for k in range(base - 1):
        index = (lane // base) * base + k
        factor = jnp.concatenate(
            [jnp.take_along_axis(packed[:, h * HALF : (h + 1) * HALF], index, axis=1) for h in range(2)], axis=1
        )
        inverse = inverse - factor * inverse[k : k + 1, :]
    inverse = jnp.where(on_diag, jnp.concatenate([inverse] * blocks, axis=0), 0.0)
    size = base
    while size < NB:
        same = (row // (2 * size)) == (col // (2 * size))
        below = same & ((row // size) % 2 == 1) & ((col // size) % 2 == 0)
        corner = jnp.where(below, lower, 0.0)
        parts = split(inverse)
        inverse = inverse - dot3(parts, split(dot3(split(corner), parts)))
        size *= 2
    return inverse


def update_kernel(piv, slab, pt, gathered, diag, out, rows, leading, upper_t, result, load_sem, store_sem):
    p = lax.axis_index("prow")
    load = pltpu.make_async_copy(slab, rows.at[pl.ds(0, ROWS)], load_sem)
    load.start()

    for h in range(2):
        for z in range(NZ):
            upper_t[z * 16 : (z + 1) * 16, h * HALF : (h + 1) * HALF] = diag[h, pl.ds(z, 16, stride=NZ), :]
    row = lax.broadcasted_iota(jnp.int32, (NB, NB), 0)
    col = lax.broadcasted_iota(jnp.int32, (NB, NB), 1)
    lower = jnp.where(row > col, upper_t[...].T, 0.0)
    inverse = invert(lower)
    pivot_rows = jnp.concatenate([gathered[h, :, 0].reshape(NB, HALF) for h in range(2)], axis=1)
    upper = dot3(split(inverse), split(pivot_rows))
    upper_parts = split(upper)

    load.wait()

    def swap(k, carry):
        local = piv[k] - p * ROWS
        held = (local >= 0) & (local < ROWS)
        target = jnp.where(held, local, ROWS)
        rows[pl.ds(target, 1), :] = leading[pl.ds(k, 1), :]
        return carry

    for h in range(2):
        leading[:, h * HALF : (h + 1) * HALF] = gathered[h, :, 1].reshape(NB, HALF)
    lax.fori_loop(0, NB, swap, 0, unroll=8)

    chunk = 256
    for n in range(ROWS // chunk):
        block = pt[:, n * chunk : (n + 1) * chunk]
        product = dot3(split(block), upper_parts, (((0,), (0,)), ((), ())))
        value = rows[n * chunk : (n + 1) * chunk, :] - product
        if n == 0:
            value = jnp.where(p == 0, upper, value)
        result[n * chunk : (n + 1) * chunk, :] = value
        pltpu.make_async_copy(
            result.at[pl.ds(n * chunk, chunk)], out.at[pl.ds(n * chunk, chunk)], store_sem.at[n]
        ).start()
    for n in range(ROWS // chunk):
        pltpu.make_async_copy(
            result.at[pl.ds(n * chunk, chunk)], out.at[pl.ds(n * chunk, chunk)], store_sem.at[n]
        ).wait()


def finish(slab, pivots, pt, gathered, diag):
    vmem = pl.BlockSpec(memory_space=pltpu.VMEM)
    hbm = pl.BlockSpec(memory_space=pl.ANY)
    return pl.pallas_call(
        update_kernel,
        name="finish",
        out_shape=jax.ShapeDtypeStruct((ROWS, COLS), F32),
        in_specs=[pl.BlockSpec(memory_space=pltpu.SMEM), hbm, vmem, vmem, vmem],
        out_specs=hbm,
        scratch_shapes=[
            pltpu.VMEM((ROWS + 8, COLS), F32),
            pltpu.VMEM((NB, COLS), F32),
            pltpu.VMEM((NB, NB), F32),
            pltpu.VMEM((ROWS, COLS), F32),
            pltpu.SemaphoreType.DMA,
            pltpu.SemaphoreType.DMA((4,)),
        ],
        compiler_params=pltpu.CompilerParams(vmem_limit_bytes=32 * 1024 * 1024),
    )(pivots, slab, pt.reshape(NZ * WIDTH, ROWS), gathered, diag.reshape(2, NB, HALF))


def local(slab, panel, pivots):
    pt, gathered, diag = exchange(slab, panel.T, pivots)
    return finish(slab, pivots, pt, gathered, diag)


def solution(mesh):
    return jax.shard_map(
        local,
        mesh=mesh,
        in_specs=(P("prow", "pcol"), P("prow", "pcol"), P()),
        out_specs=P("prow", "pcol"),
        check_vma=False,
    )
```

```python
import jax
import jax.numpy as jnp
from jax import lax
from jax.experimental import pallas as pl
from jax.experimental.pallas import tpu as pltpu
from jax.sharding import PartitionSpec as P

MESH = pl.DeviceIdType.MESH
F32 = jnp.float32
BF16 = jnp.bfloat16
NB = 256
ROWS = 1024
COLS = 256
NZ = 16
CHIPS = 16
HALF = 128
WIDTH = 16
LAST = 8
REACH = 4
CHUNK = 256
BASE = 32


def exchange_kernel(
    pivots, pivot_row, slab, panel, out,
    pt, gathered, wide, piv, pivot_lanes, upper_t, leading, panel_high, panel_low, rows, masked, from_sibling, landed, mine, lead_in, piece, piece_in, column,
    local_sem, ring_send, ring_recv, a_send, a_recv, near_send, near_recv, far_send, far_recv, c_send, c_recv,
    lead_send, lead_recv, p_send, p_recv, rs_send, rs_recv, ag_send, ag_recv, sib_send, sib_recv, store_sem,
):
    p = lax.axis_index("prow")
    z = lax.axis_index("pcol")
    chip = lax.div(p, 2)
    core = lax.rem(p, 2)
    sibling = 2 * chip + 1 - core
    is_root = p == 0
    outer = (core == 1) & (chip > 0)

    def loop(first, last, act):
        def body(o, carry):
            act(o)
            return carry
        lax.fori_loop(first, last, body, 0)

    def near(o):
        return 2 * lax.rem(chip + o, CHIPS) + core

    def above(o):
        return lax.rem(z + o + NZ, NZ)

    barrier = pltpu.get_barrier_semaphore()

    def greet(device):
        pl.semaphore_signal(barrier, inc=1, device_id=device, device_id_type=MESH)

    pivot_copy = pltpu.make_async_copy(pivots, piv, local_sem.at[2])
    panel_copy = pltpu.make_async_copy(panel, pt.at[z], local_sem.at[0])
    slab_copy = pltpu.make_async_copy(slab, rows, local_sem.at[1])
    lanes_copy = pltpu.make_async_copy(pivot_row, pivot_lanes, local_sem.at[3])
    pivot_copy.start()
    lanes_copy.start()
    panel_copy.start()
    slab_copy.start()

    for o in range(1, REACH + 1):
        greet((p, above(o)))
        greet((p, above(-o)))
    loop(1, CHIPS, lambda o: greet((near(o), z)))
    greet((sibling, z))

    @pl.when(is_root)
    def _():
        loop(1, CHIPS, lambda o: greet((2 * o + 1, z)))

    @pl.when(outer)
    def _():
        greet((0, z))

    panel_copy.wait()
    for k in range(WIDTH):
        for h in range(2):
            piece[2 * k + h] = pt[z, k : k + 1, h * HALF : (h + 1) * HALF]
    pivot_copy.wait()
    lanes_copy.wait()
    slab_copy.wait()

    row_start = p * ROWS

    def pick(k, carry):
        local = piv[k] - row_start
        held = (local >= 0) & (local < ROWS)
        row = rows[pl.ds(jnp.clip(local, 0, ROWS - 1), 1), :]
        row = jnp.where(held, row, 0.0)
        masked[0, pl.ds(k, 1), :] = row[:, :HALF]
        masked[1, pl.ds(k, 1), :] = row[:, HALF:]
        return carry

    lax.fori_loop(0, NB, pick, 0, unroll=8)

    greeted = 2 * REACH + CHIPS
    pl.semaphore_wait(barrier, greeted + jnp.where(is_root, CHIPS - 1, jnp.where(outer, 1, 0)))

    def remote(src, dst, send, recv, device):
        return pltpu.make_async_remote_copy(
            src_ref=src, dst_ref=dst, send_sem=send, recv_sem=recv, device_id=device, device_id_type=MESH
        )

    def ring_copy(direction, place, half):
        jump = 2 - place % 2
        part = pt.at[above(-direction * (place - jump)), pl.ds(8 * half, 8)]
        d = (direction + 1) // 2
        return remote(
            part, part, ring_send.at[d, place, half], ring_recv.at[d, place, half], (p, above(direction * jump))
        )

    def ring_uses(direction, place, half):
        return place < LAST or (place == LAST and half == (0 if direction == 1 else 1))

    ring_legs = [(d, h) for h in range(2) for d in (1, -1)]

    def ring_pass(place):
        for d, h in ring_legs:
            if place > 0 and ring_uses(d, place, h):
                ring_copy(d, place, h).wait_recv()
            if place % 2 == 0:
                for later in (place + 2, place + 1):
                    if ring_uses(d, later, h):
                        ring_copy(d, later, h).start()

    def a_copy(target):
        return remote(piece.at[target], piece_in.at[z], a_send, a_recv, (target, z))

    def lead_copy(target):
        t_chip, t_core = lax.div(target, 2), lax.rem(target, 2)
        src = rows.at[pl.ds(t_chip * 16, 16), pl.ds(pl.multiple_of(t_core * HALF, HALF), HALF)]
        return remote(src, lead_in, lead_send, lead_recv, (target, z))

    def rs_copy(o):
        t_chip = lax.rem(chip + o, CHIPS)
        return remote(masked.at[2, pl.ds(t_chip * 16, 16)], landed.at[o], rs_send, rs_recv, (near(o), z))

    def ag_copy(o):
        return remote(mine, gathered.at[core, chip], ag_send, ag_recv, (near(o), z))

    def c_copy(o):
        return remote(column, wide.at[core, pl.ds(pl.multiple_of(16 * chip, 16), 16)], c_send, c_recv, (near(o), z))

    def b_copy(source, to, send, recv):
        part = piece_in.at[above(source)]
        return remote(part, part, send, recv, (p, above(to)))

    sib_p = remote(masked.at[1 - core], from_sibling, p_send, p_recv, (sibling, z))
    sib_g = remote(gathered.at[core], gathered.at[core], sib_send.at[0], sib_recv.at[0], (sibling, z))
    sib_d = remote(wide.at[core], wide.at[core], sib_send.at[1], sib_recv.at[1], (sibling, z))
    here = (p, z)
    rs_all = remote(masked.at[2, pl.ds(0, 15 * 16)], landed.at[pl.ds(1, 15)], rs_send, rs_recv, here)
    ag_all = remote(gathered.at[core, pl.ds(0, 15)], gathered.at[core, pl.ds(0, 15)], ag_send, ag_recv, here)
    c_all = remote(wide.at[core, pl.ds(0, 240)], wide.at[core, pl.ds(0, 240)], c_send, c_recv, here)
    near_all = remote(piece_in.at[pl.ds(0, 8)], piece_in.at[pl.ds(0, 8)], near_send, near_recv, here)
    far_all = remote(piece_in.at[pl.ds(0, 7)], piece_in.at[pl.ds(0, 7)], far_send, far_recv, here)
    lead_all = remote(rows.at[pl.ds(0, 31 * 8)], rows.at[pl.ds(0, 31 * 8)], lead_send, lead_recv, here)
    a_all = remote(piece.at[pl.ds(1, 31)], piece.at[pl.ds(1, 31)], a_send, a_recv, here)

    def a_start():
        @pl.when(is_root)
        def _():
            loop(1, 2 * CHIPS, lambda t: a_copy(t).start())
            piece_in[z] = piece[0]

    def lead_start():
        @pl.when(is_root)
        def _():
            loop(1, 2 * CHIPS, lambda t: lead_copy(t).start())
            lead_in[...] = rows[0:16, 0:HALF]

    def near_start():
        @pl.when(p > 0)
        def _():
            a_copy(p).wait_recv()
        for o in range(1, REACH + 1):
            b_copy(0, o, near_send, near_recv).start()
            b_copy(0, -o, near_send, near_recv).start()

    def far_start():
        near_all.wait_recv()
        for o in range(1, REACH + 1):
            b_copy(-o, REACH, far_send, far_recv).start()
            if o < REACH:
                b_copy(o, -REACH, far_send, far_recv).start()

    def c_start():
        far_all.wait_recv()
        for k in range(NZ):
            column[k : k + 1, :] = piece_in[k]
        wide[core, pl.ds(pl.multiple_of(16 * chip, 16), 16)] = column[...]
        loop(1, CHIPS, lambda o: c_copy(o).start())

    def d_start():
        c_all.wait_recv()
        sib_d.start()

    def rs_start():
        sib_p.wait_recv()
        masked[2] = masked[core] + from_sibling[...]
        loop(1, CHIPS, lambda o: rs_copy(o).start())

    def ag_start():
        rs_all.wait_recv()
        @pl.when(p > 0)
        def _():
            lead_copy(p).wait_recv()
        total = masked[2, pl.ds(chip * 16, 16)]
        for o in range(1, CHIPS):
            total = total + landed[o]
        mine[0] = total
        mine[1] = lead_in[...]
        gathered[core, chip] = mine[...]
        loop(1, CHIPS, lambda o: ag_copy(o).start())

    def g_start():
        ag_all.wait_recv()
        sib_g.start()

    def swap_rows():
        sib_g.wait_recv()
        for h in range(2):
            leading[:, h * HALF : (h + 1) * HALF] = gathered[h, :, 1].reshape(NB, HALF)
        lead_high, lead_low = split(leading[...])
        ones = jnp.ones((NB, COLS), BF16)
        for n in range(ROWS // CHUNK):
            index = lax.broadcasted_iota(jnp.int32, (CHUNK, NB), 0) + (row_start + n * CHUNK)
            chosen = jnp.where(index == pivot_lanes[...], 1.0, 0.0).astype(BF16)
            replaced = dot1(chosen, lead_high) + dot1(chosen, lead_low)
            part = slice(n * CHUNK, (n + 1) * CHUNK)
            rows[part, :] = jnp.where(dot1(chosen, ones) > 0.5, replaced, rows[part, :])

    def split_panel():
        for n in range(ROWS // CHUNK):
            part = slice(n * CHUNK, (n + 1) * CHUNK)
            high, low = split(pt[:, :, part].reshape(NB, CHUNK).T)
            panel_high[part, :] = high
            panel_low[part, :] = low

    a_start()
    sib_p.start()
    ring_pass(0)
    lead_start()
    rs_start()
    near_start()
    ring_pass(2)
    ag_start()
    far_start()
    ring_pass(4)
    ring_pass(1)
    c_start()
    ring_pass(6)
    g_start()
    ring_pass(3)
    @pl.when(is_root)
    def _():
        lead_all.wait_send()
    d_start()
    swap_rows()
    for place in (5, 7, 8):
        ring_pass(place)
    split_panel()
    sib_d.wait_recv()

    for h in range(2):
        for k in range(NZ):
            upper_t[k * 16 : (k + 1) * 16, h * HALF : (h + 1) * HALF] = wide[h, pl.ds(k, 16, stride=NZ), :]
    first, second = slice(0, HALF), slice(HALF, NB)
    corner = split(upper_t[first, second].T)
    top = split(invert(upper_t[first, first].T))
    bottom = split(invert(upper_t[second, second].T))

    def pivot_half(h):
        return jnp.concatenate([gathered[c, 8 * h : 8 * h + 8, 0].reshape(HALF, HALF) for c in range(2)], axis=1)

    upper_first = dot3(top, split(pivot_half(0)))
    upper_second = dot3(bottom, split(pivot_half(1) - dot3(corner, split(upper_first))))
    upper = jnp.concatenate([upper_first, upper_second], axis=0)
    upper_parts = split(upper)

    def store(n):
        part = pl.ds(n * CHUNK, CHUNK)
        return pltpu.make_async_copy(rows.at[part], out.at[part], store_sem.at[n])

    for n in range(ROWS // CHUNK):
        part = slice(n * CHUNK, (n + 1) * CHUNK)
        value = rows[part, :] - dot3((panel_high[part, :], panel_low[part, :]), upper_parts)
        if n == 0:
            value = jnp.where(is_root, upper, value)
        rows[part, :] = value
        store(n).start()

    for copy in (sib_p, sib_g, sib_d, rs_all, ag_all, c_all, near_all, far_all):
        copy.wait_send()
    for place in range(1, LAST + 1):
        for d, h in ring_legs:
            if ring_uses(d, place, h):
                ring_copy(d, place, h).wait_send()

    @pl.when(is_root)
    def _():
        a_all.wait_send()

    for n in range(ROWS // CHUNK):
        store(n).wait()


def split(a):
    high = a.astype(BF16)
    return high, (a - high.astype(F32)).astype(BF16)


def dot1(a, b):
    return jnp.dot(a, b, preferred_element_type=F32)


def dot3(a, b):
    return dot1(a[0], b[0]) + (dot1(a[0], b[1]) + dot1(a[1], b[0]))


def invert(square):
    row = lax.broadcasted_iota(jnp.int32, (HALF, HALF), 0)
    col = lax.broadcasted_iota(jnp.int32, (HALF, HALF), 1)
    lower = jnp.where(row > col, square, 0.0)
    blocks = HALF // BASE
    on_diag = (row // BASE) == (col // BASE)
    packed = jnp.sum(jnp.where(on_diag, lower, 0.0).reshape(blocks, BASE, HALF), axis=0)
    small_row = lax.broadcasted_iota(jnp.int32, (BASE, HALF), 0)
    small_col = lax.broadcasted_iota(jnp.int32, (BASE, HALF), 1)
    inverse = jnp.where(small_row == small_col % BASE, 1.0, 0.0)
    for k in range(BASE - 1):
        factor = jnp.take_along_axis(packed, (small_col // BASE) * BASE + k, axis=1)
        inverse = inverse - factor * inverse[k : k + 1, :]
    inverse = jnp.where(on_diag, jnp.concatenate([inverse] * blocks, axis=0), 0.0)
    size = BASE
    while size < HALF:
        same = (row // (2 * size)) == (col // (2 * size))
        below = same & ((row // size) % 2 == 1) & ((col // size) % 2 == 0)
        parts = split(inverse)
        inverse = inverse - dot3(parts, split(dot3(split(jnp.where(below, lower, 0.0)), parts)))
        size *= 2
    return inverse


def local(slab, panel, pivots):
    dma = pltpu.SemaphoreType.DMA
    hbm = pl.BlockSpec(memory_space=pltpu.HBM)
    return pl.pallas_call(
        exchange_kernel,
        name="exchange",
        out_shape=jax.ShapeDtypeStruct((ROWS, COLS), F32),
        in_specs=[hbm] * 4,
        out_specs=hbm,
        scratch_shapes=[
            pltpu.VMEM((NZ, WIDTH, ROWS), F32),
            pltpu.VMEM((2, CHIPS, 2, 16, HALF), F32),
            pltpu.VMEM((2, NB, HALF), F32),
            pltpu.SMEM((NB,), jnp.int32),
            pltpu.VMEM((1, NB), jnp.int32),
            pltpu.VMEM((NB, NB), F32),
            pltpu.VMEM((NB, COLS), F32),
            pltpu.VMEM((ROWS, NB), BF16),
            pltpu.VMEM((ROWS, NB), BF16),
            pltpu.VMEM((ROWS, COLS), F32),
            pltpu.VMEM((3, NB, HALF), F32),
            pltpu.VMEM((NB, HALF), F32),
            pltpu.VMEM((CHIPS, 16, HALF), F32),
            pltpu.VMEM((2, 16, HALF), F32),
            pltpu.VMEM((16, HALF), F32),
            pltpu.VMEM((2 * CHIPS, 1, HALF), F32),
            pltpu.VMEM((NZ, 1, HALF), F32),
            pltpu.VMEM((NZ, HALF), F32),
            dma((4,)),
            dma((2, LAST + 1, 2)), dma((2, LAST + 1, 2)),
            dma, dma,
            dma, dma,
            dma, dma,
            dma, dma,
            dma, dma,
            dma, dma,
            dma, dma,
            dma, dma,
            dma((2,)), dma((2,)),
            dma((ROWS // CHUNK,)),
        ],
        compiler_params=pltpu.CompilerParams(
            collective_id=0, has_side_effects=True, vmem_limit_bytes=63 * 1000 * 1024
        ),
    )(pivots, pivots.reshape(1, NB), slab, panel.T)


def solution(mesh):
    return jax.shard_map(
        local,
        mesh=mesh,
        in_specs=(P("prow", "pcol"), P("prow", "pcol"), P()),
        out_specs=P("prow", "pcol"),
        check_vma=False,
    )
```

```python
import jax
import jax.numpy as jnp
from jax import lax
from jax.experimental import pallas as pl
from jax.experimental.pallas import tpu as pltpu
from jax.sharding import PartitionSpec as P

MESH = pl.DeviceIdType.MESH
F32 = jnp.float32
BF16 = jnp.bfloat16
NB = 256
ROWS = 1024
COLS = 256
NZ = 16
CHIPS = 16
HALF = 128
WIDTH = 16
LAST = 8
REACH = 4
CHUNK = 256
BASE = 32


def exchange_kernel(
    pivots, pivot_row, slab, panel, out,
    pt, gathered, wide, piv, pivot_lanes, upper_t, leading, panel_high, panel_low, rows, masked, from_sibling, landed, mine, lead_in, piece, piece_in, column,
    local_sem, ring_send, ring_recv, a_send, a_recv, b_send, b_recv, c_send, c_recv,
    lead_send, lead_recv, p_send, p_recv, rs_send, rs_recv, ag_send, ag_recv, g_send, g_recv, store_sem, known,
):
    p = lax.axis_index("prow")
    z = lax.axis_index("pcol")
    chip = lax.div(p, 2)
    core = lax.rem(p, 2)
    sibling = 2 * chip + 1 - core
    is_root = p == 0
    outer = (core == 1) & (chip > 0)

    def loop(first, last, act):
        def body(o, carry):
            act(o)
            return carry
        lax.fori_loop(first, last, body, 0)

    def near(o):
        return 2 * lax.rem(chip + o, CHIPS) + core

    def above(o):
        return lax.rem(z + o + NZ, NZ)

    x, y = lax.div(chip, 4), lax.rem(chip, 4)
    x_odd, y_odd = lax.rem(x, 2), lax.rem(y, 2)
    across, along = 4 - 8 * x_odd, 1 - 2 * y_odd
    square = [(chip + move, c) for move in (across + along, across, along) for c in (core, 1 - core)]
    square.append((chip, 1 - core))

    def part_of(target):
        target_chip = lax.div(target, 2)
        return 4 * lax.rem(lax.div(target_chip, 4), 2) + 2 * lax.rem(target_chip, 2) + lax.rem(target, 2)

    mine_part = lax.div(part_of(p), 2)
    relay = pl.ds(pl.multiple_of(core * NB + 64 * mine_part, 64), 64)

    barrier = pltpu.get_barrier_semaphore()

    def greet(device):
        pl.semaphore_signal(barrier, inc=1, device_id=device, device_id_type=MESH)

    pivot_copy = pltpu.make_async_copy(pivots, piv, local_sem.at[2])
    panel_copy = pltpu.make_async_copy(panel, pt.at[z], local_sem.at[0])
    slab_copy = pltpu.make_async_copy(slab, rows, local_sem.at[1])
    lanes_copy = pltpu.make_async_copy(pivot_row, pivot_lanes, local_sem.at[3])
    pivot_copy.start()
    lanes_copy.start()
    panel_copy.start()
    slab_copy.start()

    for o in range(1, REACH + 1):
        greet((p, above(o)))
        greet((p, above(-o)))
    loop(1, CHIPS, lambda o: greet((near(o), z)))
    for other, c in square[1::2]:
        greet((2 * other + c, z))
    greet((sibling, z))

    @pl.when(is_root)
    def _():
        loop(1, CHIPS, lambda o: greet((2 * o + 1, z)))

    @pl.when(outer)
    def _():
        greet((0, z))

    panel_copy.wait()
    for k in range(WIDTH):
        for h in range(2):
            piece[2 * (k % 4) + h, k // 4 : k // 4 + 1, :] = pt[z, k : k + 1, h * HALF : (h + 1) * HALF]
    pivot_copy.wait()
    lanes_copy.wait()
    slab_copy.wait()

    row_start = p * ROWS

    def pick(k, carry):
        local = piv[k] - row_start
        held = (local >= 0) & (local < ROWS)
        row = rows[pl.ds(jnp.clip(local, 0, ROWS - 1), 1), :]
        row = jnp.where(held, row, 0.0)
        masked[0, pl.ds(k, 1), :] = row[:, :HALF]
        masked[1, pl.ds(k, 1), :] = row[:, HALF:]
        return carry

    lax.fori_loop(0, NB, pick, 0, unroll=8)

    greeted = 2 * REACH + CHIPS + 3
    pl.semaphore_wait(barrier, greeted + jnp.where(is_root, CHIPS - 1, jnp.where(outer, 1, 0)))

    for o in (REACH, -REACH):
        pl.semaphore_signal(known, inc=1, device_id=(p, above(o)), device_id_type=MESH)

    def remote(src, dst, send, recv, device):
        return pltpu.make_async_remote_copy(
            src_ref=src, dst_ref=dst, send_sem=send, recv_sem=recv, device_id=device, device_id_type=MESH
        )

    def ring_copy(direction, place, half):
        jump = 2 - place % 2
        part = pt.at[above(-direction * (place - jump)), pl.ds(8 * half, 8)]
        d = (direction + 1) // 2
        return remote(
            part, part, ring_send.at[d, place, half], ring_recv.at[d, place, half], (p, above(direction * jump))
        )

    def ring_uses(direction, place, half):
        return place < LAST or (place == LAST and half == (0 if direction == 1 else 1))

    ring_legs = [(d, h) for h in range(2) for d in (1, -1)]

    def ring_pass(place):
        for d, h in ring_legs:
            if place > 0 and ring_uses(d, place, h):
                ring_copy(d, place, h).wait_recv()
            if place % 2 == 0:
                for later in (place + 2, place + 1):
                    if ring_uses(d, later, h):
                        ring_copy(d, later, h).start()

    def a_copy(target):
        return remote(piece.at[part_of(target)], piece_in.at[z], a_send, a_recv, (target, z))

    def lead_copy(target):
        t_chip, t_core = lax.div(target, 2), lax.rem(target, 2)
        src = rows.at[pl.ds(t_chip * 16, 16), pl.ds(pl.multiple_of(t_core * HALF, HALF), HALF)]
        return remote(src, lead_in, lead_send, lead_recv, (target, z))

    def rs_copy(o):
        t_chip = lax.rem(chip + o, CHIPS)
        return remote(masked.at[2, pl.ds(t_chip * 16, 16)], landed.at[o], rs_send, rs_recv, (near(o), z))

    def ag_copy(o):
        return remote(mine, gathered.at[core, chip], ag_send, ag_recv, (near(o), z))

    def b_copy(o):
        return remote(piece_in.at[z], piece_in.at[z], b_send, b_recv, (p, above(o)))

    sib_p = remote(masked.at[1 - core], from_sibling, p_send, p_recv, (sibling, z))
    sib_g = remote(gathered.at[core], gathered.at[core], g_send, g_recv, (sibling, z))
    c_copies = [remote(wide.at[relay], wide.at[relay], c_send, c_recv, (2 * other + c, z)) for other, c in square]
    here = (p, z)
    rs_all = remote(masked.at[2, pl.ds(0, 15 * 16)], landed.at[pl.ds(1, 15)], rs_send, rs_recv, here)
    ag_all = remote(gathered.at[core, pl.ds(0, 15)], gathered.at[core, pl.ds(0, 15)], ag_send, ag_recv, here)
    c_all = remote(wide.at[pl.ds(0, 448)], wide.at[pl.ds(0, 448)], c_send, c_recv, here)
    b_all = remote(piece_in.at[pl.ds(0, 15)], piece_in.at[pl.ds(0, 15)], b_send, b_recv, here)
    lead_all = remote(rows.at[pl.ds(0, 31 * 8)], rows.at[pl.ds(0, 31 * 8)], lead_send, lead_recv, here)
    a_all = remote(masked.at[0, pl.ds(0, 124)], masked.at[0, pl.ds(0, 124)], a_send, a_recv, here)

    def a_start():
        @pl.when(is_root)
        def _():
            loop(1, 2 * CHIPS, lambda t: a_copy(t).start())
            piece_in[z] = piece[0]

    def lead_start():
        @pl.when(is_root)
        def _():
            loop(1, 2 * CHIPS, lambda t: lead_copy(t).start())
            lead_in[...] = rows[0:16, 0:HALF]

    def b_start():
        @pl.when(p > 0)
        def _():
            a_copy(p).wait_recv()
        pl.semaphore_wait(known, 2)
        for o in (8, 7, 9, 6, 10, 5, 11, 4, 12, 3, 13, 2, 14, 1, 15):
            b_copy(o).start()

    def c_start():
        b_all.wait_recv()
        for k in range(NZ):
            column[4 * k : 4 * k + 4, :] = piece_in[k]
        wide[relay, :] = column[...]
        for copy in c_copies:
            copy.start()

    def rs_start():
        sib_p.wait_recv()
        masked[2] = masked[core] + from_sibling[...]
        loop(1, CHIPS, lambda o: rs_copy(o).start())

    def ag_start():
        rs_all.wait_recv()
        @pl.when(p > 0)
        def _():
            lead_copy(p).wait_recv()
        total = masked[2, pl.ds(chip * 16, 16)]
        for o in range(1, CHIPS):
            total = total + landed[o]
        mine[0] = total
        mine[1] = lead_in[...]
        gathered[core, chip] = mine[...]
        loop(1, CHIPS, lambda o: ag_copy(o).start())

    def g_start():
        ag_all.wait_recv()
        sib_g.start()

    def swap_rows():
        sib_g.wait_recv()
        for h in range(2):
            leading[:, h * HALF : (h + 1) * HALF] = gathered[h, :, 1].reshape(NB, HALF)
        lead_high, lead_low = split(leading[...])
        ones = jnp.ones((NB, COLS), BF16)
        for n in range(ROWS // CHUNK):
            index = lax.broadcasted_iota(jnp.int32, (CHUNK, NB), 0) + (row_start + n * CHUNK)
            chosen = jnp.where(index == pivot_lanes[...], 1.0, 0.0).astype(BF16)
            replaced = dot1(chosen, lead_high) + dot1(chosen, lead_low)
            part = slice(n * CHUNK, (n + 1) * CHUNK)
            rows[part, :] = jnp.where(dot1(chosen, ones) > 0.5, replaced, rows[part, :])

    def split_blocks(*places):
        for place in places:
            block = above(place)
            high, low = split(pt[block])
            part = pl.ds(pl.multiple_of(WIDTH * block, WIDTH), WIDTH)
            panel_high[part, :] = high
            panel_low[part, :] = low

    a_start()
    sib_p.start()
    ring_pass(0)
    lead_start()
    rs_start()
    b_start()
    ring_pass(2)
    split_blocks(0, 2, -2)
    ag_start()
    ring_pass(4)
    ring_pass(1)
    split_blocks(4, -4, 1, -1)
    c_start()
    ring_pass(6)
    g_start()
    ring_pass(3)
    split_blocks(3, -3, 6, -6)
    @pl.when(is_root)
    def _():
        lead_all.wait_send()
    swap_rows()
    c_all.wait_recv()

    for h in range(2):
        for g in range(4):
            upper_t[pl.ds(h * NB + g, 64, stride=4), :] = wide[h * NB + 64 * g : h * NB + 64 * g + 64, :]
    corner = split(upper_t[NB : NB + HALF, :].T)
    top = split(invert(upper_t[0:HALF, :].T))
    bottom = split(invert(upper_t[NB + HALF : 2 * NB, :].T))

    def pivot_half(h):
        return jnp.concatenate([gathered[c, 8 * h : 8 * h + 8, 0].reshape(HALF, HALF) for c in range(2)], axis=1)

    upper_first = dot3(top, split(pivot_half(0)))
    upper_second = dot3(bottom, split(pivot_half(1) - dot3(corner, split(upper_first))))
    upper = jnp.concatenate([upper_first, upper_second], axis=0)
    upper_parts = split(upper)

    for place in (5, 7, 8):
        ring_pass(place)
    split_blocks(5, -5, 7, -7, 8)

    def store(n):
        part = pl.ds(n * CHUNK, CHUNK)
        return pltpu.make_async_copy(rows.at[part], out.at[part], store_sem.at[n])

    for n in range(ROWS // CHUNK):
        part = slice(n * CHUNK, (n + 1) * CHUNK)
        value = rows[part, :] - dot3((panel_high[:, part], panel_low[:, part]), upper_parts, 0)
        if n == 0:
            value = jnp.where(is_root, upper, value)
        rows[part, :] = value
        store(n).start()

    for copy in (sib_p, sib_g, rs_all, ag_all, b_all, c_all):
        copy.wait_send()
    for place in range(1, LAST + 1):
        for d, h in ring_legs:
            if ring_uses(d, place, h):
                ring_copy(d, place, h).wait_send()

    @pl.when(is_root)
    def _():
        a_all.wait_send()

    for n in range(ROWS // CHUNK):
        store(n).wait()


def split(a):
    high = a.astype(BF16)
    return high, (a - high.astype(F32)).astype(BF16)


def dot1(a, b, dim=1):
    return lax.dot_general(a, b, (((dim,), (0,)), ((), ())), preferred_element_type=F32)


def dot3(a, b, dim=1):
    return dot1(a[0], b[0], dim) + (dot1(a[0], b[1], dim) + dot1(a[1], b[0], dim))


def invert(square):
    row = lax.broadcasted_iota(jnp.int32, (HALF, HALF), 0)
    col = lax.broadcasted_iota(jnp.int32, (HALF, HALF), 1)
    lower = jnp.where(row > col, square, 0.0)
    blocks = HALF // BASE
    on_diag = (row // BASE) == (col // BASE)
    packed = jnp.sum(jnp.where(on_diag, lower, 0.0).reshape(blocks, BASE, HALF), axis=0)
    small_row = lax.broadcasted_iota(jnp.int32, (BASE, HALF), 0)
    small_col = lax.broadcasted_iota(jnp.int32, (BASE, HALF), 1)
    inverse = jnp.where(small_row == small_col % BASE, 1.0, 0.0)
    for k in range(BASE - 1):
        factor = jnp.take_along_axis(packed, (small_col // BASE) * BASE + k, axis=1)
        inverse = inverse - factor * inverse[k : k + 1, :]
    inverse = jnp.where(on_diag, jnp.concatenate([inverse] * blocks, axis=0), 0.0)
    size = BASE
    while size < HALF:
        same = (row // (2 * size)) == (col // (2 * size))
        below = same & ((row // size) % 2 == 1) & ((col // size) % 2 == 0)
        parts = split(inverse)
        inverse = inverse - dot3(parts, split(dot3(split(jnp.where(below, lower, 0.0)), parts)))
        size *= 2
    return inverse


def local(slab, panel, pivots):
    dma = pltpu.SemaphoreType.DMA
    hbm = pl.BlockSpec(memory_space=pltpu.HBM)
    return pl.pallas_call(
        exchange_kernel,
        name="exchange",
        out_shape=jax.ShapeDtypeStruct((ROWS, COLS), F32),
        in_specs=[hbm] * 4,
        out_specs=hbm,
        scratch_shapes=[
            pltpu.VMEM((NZ, WIDTH, ROWS), F32),
            pltpu.VMEM((2, CHIPS, 2, 16, HALF), F32),
            pltpu.VMEM((2 * NB, HALF), F32),
            pltpu.SMEM((NB,), jnp.int32),
            pltpu.VMEM((1, NB), jnp.int32),
            pltpu.VMEM((2 * NB, HALF), F32),
            pltpu.VMEM((NB, COLS), F32),
            pltpu.VMEM((NB, ROWS), BF16),
            pltpu.VMEM((NB, ROWS), BF16),
            pltpu.VMEM((ROWS, COLS), F32),
            pltpu.VMEM((3, NB, HALF), F32),
            pltpu.VMEM((NB, HALF), F32),
            pltpu.VMEM((CHIPS, 16, HALF), F32),
            pltpu.VMEM((2, 16, HALF), F32),
            pltpu.VMEM((16, HALF), F32),
            pltpu.VMEM((8, 4, HALF), F32),
            pltpu.VMEM((NZ, 4, HALF), F32),
            pltpu.VMEM((4 * NZ, HALF), F32),
            dma((4,)),
            dma((2, LAST + 1, 2)), dma((2, LAST + 1, 2)),
            dma, dma,
            dma, dma,
            dma, dma,
            dma, dma,
            dma, dma,
            dma, dma,
            dma, dma,
            dma, dma,
            dma((ROWS // CHUNK,)),
            pltpu.SemaphoreType.REGULAR,
        ],
        compiler_params=pltpu.CompilerParams(
            collective_id=0, has_side_effects=True, vmem_limit_bytes=63 * 1000 * 1024
        ),
    )(pivots, pivots.reshape(1, NB), slab, panel.T)


def solution(mesh):
    return jax.shard_map(
        local,
        mesh=mesh,
        in_specs=(P("prow", "pcol"), P("prow", "pcol"), P()),
        out_specs=P("prow", "pcol"),
        check_vma=False,
    )
```

```python
import jax
import jax.numpy as jnp
from jax import lax
from jax.experimental import pallas as pl
from jax.experimental.pallas import tpu as pltpu
from jax.sharding import PartitionSpec as P

MESH = pl.DeviceIdType.MESH
F32 = jnp.float32
BF16 = jnp.bfloat16
NB = 256
ROWS = 1024
COLS = 256
NZ = 16
CHIPS = 16
HALF = 128
WIDTH = 16
LAST = 8
REACH = 4
CHUNK = 256
BASE = 32


def exchange_kernel(
    pivots, pivot_row, slab, panel, out,
    pt, gathered, wide, piv, pivot_lanes, upper_t, leading, panel_high, panel_low, rows, masked, from_sibling, landed, mine, lead_in, piece, piece_in, column,
    local_sem, ring_send, ring_recv, a_send, a_recv, b_send, b_recv, c_send, c_recv,
    lead_send, lead_recv, p_send, p_recv, rs_send, rs_recv, ag_send, ag_recv, g_send, g_recv, known,
):
    p = lax.axis_index("prow")
    z = lax.axis_index("pcol")
    chip = lax.div(p, 2)
    core = lax.rem(p, 2)
    sibling = 2 * chip + 1 - core
    is_root = p == 0
    outer = (core == 1) & (chip > 0)

    def loop(first, last, act):
        def body(o, carry):
            act(o)
            return carry
        lax.fori_loop(first, last, body, 0)

    def near(o):
        return 2 * lax.rem(chip + o, CHIPS) + core

    def above(o):
        return lax.rem(z + o + NZ, NZ)

    x, y = lax.div(chip, 4), lax.rem(chip, 4)
    x_odd, y_odd = lax.rem(x, 2), lax.rem(y, 2)
    across, along = 4 - 8 * x_odd, 1 - 2 * y_odd
    square = [(chip + move, c) for move in (across + along, across, along) for c in (core, 1 - core)]
    square.append((chip, 1 - core))

    def part_of(target):
        target_chip = lax.div(target, 2)
        return 4 * lax.rem(lax.div(target_chip, 4), 2) + 2 * lax.rem(target_chip, 2) + lax.rem(target, 2)

    mine_part = lax.div(part_of(p), 2)
    relay = pl.ds(pl.multiple_of(core * NB + 64 * mine_part, 64), 64)

    barrier = pltpu.get_barrier_semaphore()

    def greet(device):
        pl.semaphore_signal(barrier, inc=1, device_id=device, device_id_type=MESH)

    pivot_copy = pltpu.make_async_copy(pivots, piv, local_sem.at[2])
    panel_copy = pltpu.make_async_copy(panel, pt.at[z], local_sem.at[0])
    slab_copy = pltpu.make_async_copy(slab, rows, local_sem.at[1])
    lanes_copy = pltpu.make_async_copy(pivot_row, pivot_lanes, local_sem.at[3])
    panel_copy.start()
    slab_copy.start()
    pivot_copy.start()
    lanes_copy.start()

    for o in (10, 9, 11, 6, 14):
        greet((near(o), z))
    for o in range(REACH, 0, -1):
        greet((p, above(o)))
        greet((p, above(-o)))
    for o in (2, 5, 7, 8, 13, 15, 1, 3, 4, 12):
        greet((near(o), z))
    for other, c in square[1::2]:
        greet((2 * other + c, z))
    greet((sibling, z))

    @pl.when(is_root)
    def _():
        loop(1, CHIPS, lambda o: greet((2 * o + 1, z)))

    @pl.when(outer)
    def _():
        greet((0, z))

    panel_copy.wait()
    for k in range(WIDTH):
        for h in range(2):
            piece[2 * (k % 4) + h, k // 4 : k // 4 + 1, :] = pt[z, k : k + 1, h * HALF : (h + 1) * HALF]
    pivot_copy.wait()
    lanes_copy.wait()
    slab_copy.wait()

    row_start = p * ROWS

    def pick(k, carry):
        local = piv[k] - row_start
        held = (local >= 0) & (local < ROWS)
        row = rows[pl.ds(jnp.clip(local, 0, ROWS - 1), 1), :]
        row = jnp.where(held, row, 0.0)
        masked[0, pl.ds(k, 1), :] = row[:, :HALF]
        masked[1, pl.ds(k, 1), :] = row[:, HALF:]
        return carry

    lax.fori_loop(0, NB, pick, 0, unroll=8)

    greeted = 2 * REACH + CHIPS + 3
    pl.semaphore_wait(barrier, greeted + jnp.where(is_root, CHIPS - 1, jnp.where(outer, 1, 0)))

    for o in (REACH, -REACH):
        pl.semaphore_signal(known, inc=1, device_id=(p, above(o)), device_id_type=MESH)

    def remote(src, dst, send, recv, device):
        return pltpu.make_async_remote_copy(
            src_ref=src, dst_ref=dst, send_sem=send, recv_sem=recv, device_id=device, device_id_type=MESH
        )

    def ring_copy(direction, place, half):
        jump = 2 - place % 2
        part = pt.at[above(-direction * (place - jump)), pl.ds(8 * half, 8)]
        d = (direction + 1) // 2
        return remote(
            part, part, ring_send.at[d, place, half], ring_recv.at[d, place, half], (p, above(direction * jump))
        )

    def ring_uses(direction, place, half):
        return place < LAST or (place == LAST and half == (0 if direction == 1 else 1))

    ring_legs = [(d, h) for h in range(2) for d in (1, -1)]

    def ring_pass(place):
        for d, h in ring_legs:
            if place > 0 and ring_uses(d, place, h):
                ring_copy(d, place, h).wait_recv()
            if place % 2 == 0:
                for later in (place + 2, place + 1):
                    if ring_uses(d, later, h):
                        ring_copy(d, later, h).start()

    def a_copy(target):
        return remote(piece.at[part_of(target)], piece_in.at[z], a_send, a_recv, (target, z))

    def lead_copy(target):
        t_chip, t_core = lax.div(target, 2), lax.rem(target, 2)
        src = rows.at[pl.ds(t_chip * 16, 16), pl.ds(pl.multiple_of(t_core * HALF, HALF), HALF)]
        return remote(src, lead_in, lead_send, lead_recv, (target, z))

    def rs_copy(o):
        t_chip = lax.rem(chip + o, CHIPS)
        return remote(masked.at[2, pl.ds(t_chip * 16, 16)], landed.at[o], rs_send, rs_recv, (near(o), z))

    def ag_copy(o):
        return remote(mine, gathered.at[core, chip], ag_send, ag_recv, (near(o), z))

    def b_copy(o):
        return remote(piece_in.at[z], piece_in.at[z], b_send, b_recv, (p, above(o)))

    sib_p = remote(masked.at[1 - core], from_sibling, p_send, p_recv, (sibling, z))
    sib_g = remote(gathered.at[core], gathered.at[core], g_send, g_recv, (sibling, z))
    c_copies = [remote(wide.at[relay], wide.at[relay], c_send, c_recv, (2 * other + c, z)) for other, c in square]
    here = (p, z)
    rs_all = remote(masked.at[2, pl.ds(0, 15 * 16)], landed.at[pl.ds(1, 15)], rs_send, rs_recv, here)
    ag_all = remote(gathered.at[core, pl.ds(0, 15)], gathered.at[core, pl.ds(0, 15)], ag_send, ag_recv, here)
    c_all = remote(wide.at[pl.ds(0, 448)], wide.at[pl.ds(0, 448)], c_send, c_recv, here)
    b_all = remote(piece_in.at[pl.ds(0, 15)], piece_in.at[pl.ds(0, 15)], b_send, b_recv, here)
    lead_all = remote(rows.at[pl.ds(0, 31 * 8)], rows.at[pl.ds(0, 31 * 8)], lead_send, lead_recv, here)
    a_all = remote(masked.at[0, pl.ds(0, 124)], masked.at[0, pl.ds(0, 124)], a_send, a_recv, here)

    def a_start():
        @pl.when(is_root)
        def _():
            loop(1, 2 * CHIPS, lambda t: a_copy(t).start())
            piece_in[z] = piece[0]

    def lead_start():
        @pl.when(is_root)
        def _():
            loop(1, 2 * CHIPS, lambda t: lead_copy(t).start())
            lead_in[...] = rows[0:16, 0:HALF]

    def b_start():
        @pl.when(p > 0)
        def _():
            a_copy(p).wait_recv()
        pl.semaphore_wait(known, 2)
        for o in (8, 7, 9, 6, 10, 5, 11, 4, 12, 3, 13, 2, 14, 1, 15):
            b_copy(o).start()

    def c_start():
        b_all.wait_recv()
        for k in range(NZ):
            column[4 * k : 4 * k + 4, :] = piece_in[k]
        wide[relay, :] = column[...]
        for copy in c_copies:
            copy.start()

    def rs_start():
        sib_p.wait_recv()
        masked[2] = masked[core] + from_sibling[...]
        loop(1, CHIPS, lambda o: rs_copy(o).start())

    def ag_start():
        rs_all.wait_recv()
        @pl.when(p > 0)
        def _():
            lead_copy(p).wait_recv()
        total = masked[2, pl.ds(chip * 16, 16)]
        for o in range(1, CHIPS):
            total = total + landed[o]
        mine[0] = total
        mine[1] = lead_in[...]
        gathered[core, chip] = mine[...]
        loop(1, CHIPS, lambda o: ag_copy(o).start())

    def g_start():
        ag_all.wait_recv()
        sib_g.start()

    def swap_rows():
        sib_g.wait_recv()
        for h in range(2):
            leading[:, h * HALF : (h + 1) * HALF] = gathered[h, :, 1].reshape(NB, HALF)
        lead_high, lead_low = split(leading[...])
        ones = jnp.ones((NB, COLS), BF16)
        for n in range(ROWS // CHUNK):
            index = lax.broadcasted_iota(jnp.int32, (CHUNK, NB), 0) + (row_start + n * CHUNK)
            chosen = jnp.where(index == pivot_lanes[...], 1.0, 0.0).astype(BF16)
            replaced = dot1(chosen, lead_high) + dot1(chosen, lead_low)
            part = slice(n * CHUNK, (n + 1) * CHUNK)
            rows[part, :] = jnp.where(dot1(chosen, ones) > 0.5, replaced, rows[part, :])

    def split_blocks(*places):
        for place in places:
            block = above(place)
            high, low = split(pt[block])
            part = pl.ds(pl.multiple_of(WIDTH * block, WIDTH), WIDTH)
            panel_high[part, :] = high
            panel_low[part, :] = low

    a_start()
    sib_p.start()
    ring_pass(0)
    lead_start()
    rs_start()
    b_start()
    ring_pass(2)
    split_blocks(0, 2, -2)
    ag_start()
    ring_pass(4)
    ring_pass(1)
    split_blocks(4, -4, 1, -1)
    c_start()
    ring_pass(6)
    g_start()
    ring_pass(3)
    split_blocks(3, -3, 6, -6)
    @pl.when(is_root)
    def _():
        lead_all.wait_send()
    swap_rows()
    c_all.wait_recv()

    for h in range(2):
        for g in range(4):
            upper_t[pl.ds(h * NB + g, 64, stride=4), :] = wide[h * NB + 64 * g : h * NB + 64 * g + 64, :]
    corner = split(upper_t[NB : NB + HALF, :].T)
    top = split(invert(upper_t[0:HALF, :].T))
    bottom = split(invert(upper_t[NB + HALF : 2 * NB, :].T))

    def pivot_half(h):
        return jnp.concatenate([gathered[c, 8 * h : 8 * h + 8, 0].reshape(HALF, HALF) for c in range(2)], axis=1)

    upper_first = dot3(top, split(pivot_half(0)))
    upper_second = dot3(bottom, split(pivot_half(1) - dot3(corner, split(upper_first))))
    upper = jnp.concatenate([upper_first, upper_second], axis=0)
    upper_parts = split(upper)

    for place in (5, 7, 8):
        ring_pass(place)
    split_blocks(5, -5, 7, -7, 8)

    for n in range(ROWS // CHUNK):
        part = slice(n * CHUNK, (n + 1) * CHUNK)
        value = rows[part, :] - dot3((panel_high[:, part], panel_low[:, part]), upper_parts, 0)
        if n == 0:
            value = jnp.where(is_root, upper, value)
        out[part, :] = value

    for copy in (sib_p, sib_g, rs_all, ag_all, b_all, c_all):
        copy.wait_send()
    for place in range(1, LAST + 1):
        for d, h in ring_legs:
            if ring_uses(d, place, h):
                ring_copy(d, place, h).wait_send()

    @pl.when(is_root)
    def _():
        a_all.wait_send()


def split(a):
    high = a.astype(BF16)
    return high, (a - high.astype(F32)).astype(BF16)


def dot1(a, b, dim=1):
    return lax.dot_general(a, b, (((dim,), (0,)), ((), ())), preferred_element_type=F32)


def dot3(a, b, dim=1):
    return dot1(a[0], b[0], dim) + (dot1(a[0], b[1], dim) + dot1(a[1], b[0], dim))


def invert(square):
    row = lax.broadcasted_iota(jnp.int32, (HALF, HALF), 0)
    col = lax.broadcasted_iota(jnp.int32, (HALF, HALF), 1)
    lower = jnp.where(row > col, square, 0.0)
    blocks = HALF // BASE
    on_diag = (row // BASE) == (col // BASE)
    packed = jnp.sum(jnp.where(on_diag, lower, 0.0).reshape(blocks, BASE, HALF), axis=0)
    small_row = lax.broadcasted_iota(jnp.int32, (BASE, HALF), 0)
    small_col = lax.broadcasted_iota(jnp.int32, (BASE, HALF), 1)
    inverse = jnp.where(small_row == small_col % BASE, 1.0, 0.0)
    for k in range(BASE - 1):
        factor = jnp.take_along_axis(packed, (small_col // BASE) * BASE + k, axis=1)
        inverse = inverse - factor * inverse[k : k + 1, :]
    inverse = jnp.where(on_diag, jnp.concatenate([inverse] * blocks, axis=0), 0.0)
    size = BASE
    while size < HALF:
        same = (row // (2 * size)) == (col // (2 * size))
        below = same & ((row // size) % 2 == 1) & ((col // size) % 2 == 0)
        parts = split(inverse)
        inverse = inverse - dot3(parts, split(dot3(split(jnp.where(below, lower, 0.0)), parts)))
        size *= 2
    return inverse


def local(slab, panel, pivots):
    dma = pltpu.SemaphoreType.DMA
    hbm = pl.BlockSpec(memory_space=pltpu.HBM)
    return pl.pallas_call(
        exchange_kernel,
        name="exchange",
        out_shape=jax.ShapeDtypeStruct((ROWS, COLS), F32),
        in_specs=[hbm] * 4,
        out_specs=pl.BlockSpec(memory_space=pltpu.VMEM),
        scratch_shapes=[
            pltpu.VMEM((NZ, WIDTH, ROWS), F32),
            pltpu.VMEM((2, CHIPS, 2, 16, HALF), F32),
            pltpu.VMEM((2 * NB, HALF), F32),
            pltpu.SMEM((NB,), jnp.int32),
            pltpu.VMEM((1, NB), jnp.int32),
            pltpu.VMEM((2 * NB, HALF), F32),
            pltpu.VMEM((NB, COLS), F32),
            pltpu.VMEM((NB, ROWS), BF16),
            pltpu.VMEM((NB, ROWS), BF16),
            pltpu.VMEM((ROWS, COLS), F32),
            pltpu.VMEM((3, NB, HALF), F32),
            pltpu.VMEM((NB, HALF), F32),
            pltpu.VMEM((CHIPS, 16, HALF), F32),
            pltpu.VMEM((2, 16, HALF), F32),
            pltpu.VMEM((16, HALF), F32),
            pltpu.VMEM((8, 4, HALF), F32),
            pltpu.VMEM((NZ, 4, HALF), F32),
            pltpu.VMEM((4 * NZ, HALF), F32),
            dma((4,)),
            dma((2, LAST + 1, 2)), dma((2, LAST + 1, 2)),
            dma, dma,
            dma, dma,
            dma, dma,
            dma, dma,
            dma, dma,
            dma, dma,
            dma, dma,
            dma, dma,
            pltpu.SemaphoreType.REGULAR,
        ],
        compiler_params=pltpu.CompilerParams(
            collective_id=0, has_side_effects=True, vmem_limit_bytes=24576 * 1024
        ),
    )(*(pltpu.with_memory_space_constraint(a, pltpu.HBM) for a in (pivots, pivots.reshape(1, NB), slab, panel.T)))


def solution(mesh):
    return jax.shard_map(
        local,
        mesh=mesh,
        in_specs=(P("prow", "pcol"), P("prow", "pcol"), P()),
        out_specs=P("prow", "pcol"),
        check_vma=False,
    )
```

```python
import jax
import jax.numpy as jnp
from jax import lax
from jax.experimental import pallas as pl
from jax.experimental.pallas import tpu as pltpu
from jax.sharding import PartitionSpec as P

MESH = pl.DeviceIdType.MESH
F32 = jnp.float32
BF16 = jnp.bfloat16
NB = 256
ROWS = 1024
COLS = 256
NZ = 16
CHIPS = 16
HALF = 128
WIDTH = 16
LAST = 8
REACH = 4
CHUNK = 256
BASE = 32


def exchange_kernel(
    pivots, pivot_row, slab, panel, out,
    pt, gathered, wide, piv, pivot_lanes, upper_t, leading, panel_high, panel_low, rows, masked, from_sibling, landed, mine, lead_in, piece, piece_in, column,
    local_sem, ring_send, ring_recv, leaf_recv, a_send, a_recv, b_send, b_recv, c_send, c_recv,
    lead_send, lead_recv, p_send, p_recv, rs_send, rs_recv, ag_send, ag_recv, g_send, g_recv, known,
):
    p = lax.axis_index("prow")
    z = lax.axis_index("pcol")
    chip = lax.div(p, 2)
    core = lax.rem(p, 2)
    sibling = 2 * chip + 1 - core
    is_root = p == 0
    outer = (core == 1) & (chip > 0)

    def wrapped(index, size):
        return jnp.where(index >= size, index - size, jnp.where(index < 0, index + size, index))

    nears = [2 * wrapped(chip + o, CHIPS) + core for o in range(CHIPS)]
    aboves = [wrapped(z + o, NZ) if o < 9 else wrapped(z + o - NZ, NZ) for o in range(NZ)]

    def near(o):
        return nears[o]

    def above(o):
        return aboves[o % NZ]

    x, y = lax.div(chip, 4), lax.rem(chip, 4)
    x_odd, y_odd = lax.rem(x, 2), lax.rem(y, 2)
    across, along = 4 - 8 * x_odd, 1 - 2 * y_odd
    square = [(chip + move, c) for move in (across + along, across, along) for c in (core, 1 - core)]
    square.append((chip, 1 - core))

    def part_of(target):
        return 4 * (target // 8 % 2) + 2 * (target // 2 % 2) + target % 2

    mine_part = 2 * x_odd + y_odd
    relay = pl.ds(pl.multiple_of(core * NB + 64 * mine_part, 64), 64)

    barrier = pltpu.get_barrier_semaphore()

    def greet(device):
        pl.semaphore_signal(barrier, inc=1, device_id=device, device_id_type=MESH)

    pivot_copy = pltpu.make_async_copy(pivots, piv, local_sem.at[2])
    panel_copy = pltpu.make_async_copy(panel, pt.at[z], local_sem.at[0])
    slab_copy = pltpu.make_async_copy(slab, rows, local_sem.at[1])
    lanes_copy = pltpu.make_async_copy(pivot_row, pivot_lanes, local_sem.at[3])
    panel_copy.start()
    slab_copy.start()
    pivot_copy.start()
    lanes_copy.start()

    for o in (10, 9, 11, 6, 14):
        greet((near(o), z))
    for o in range(REACH, 0, -1):
        greet((p, above(o)))
        greet((p, above(-o)))
    for o in (2, 5, 7, 8, 13, 15, 1, 3, 4, 12):
        greet((near(o), z))
    for other, c in square[1::2]:
        greet((2 * other + c, z))
    greet((sibling, z))

    @pl.when(is_root)
    def _():
        for o in range(1, CHIPS):
            greet((2 * o + 1, z))

    @pl.when(outer)
    def _():
        greet((0, z))

    panel_copy.wait()
    for k in range(WIDTH):
        for h in range(2):
            piece[2 * (k % 4) + h, k // 4 : k // 4 + 1, :] = pt[z, k : k + 1, h * HALF : (h + 1) * HALF]
    greeted = 2 * REACH + CHIPS + 3
    pl.semaphore_wait(barrier, greeted + jnp.where(is_root, CHIPS - 1, jnp.where(outer, 1, 0)))

    for o in (REACH, -REACH):
        pl.semaphore_signal(known, inc=1, device_id=(p, above(o)), device_id_type=MESH)

    def remote(src, dst, send, recv, device):
        return pltpu.make_async_remote_copy(
            src_ref=src, dst_ref=dst, send_sem=send, recv_sem=recv, device_id=device, device_id_type=MESH
        )

    def ring_copy(direction, place, half):
        jump = 2 - place % 2
        block = above(-direction * (place - jump))
        d = (direction + 1) // 2
        if place % 2:
            part, arrived = pt.at[block], leaf_recv.at[place // 4]
        else:
            part = pt.at[block, pl.ds(8 * half, 8)]
            arrived = leaf_recv.at[1] if place == LAST else ring_recv.at[d, place // 2 - 1, half]
        return remote(part, part, ring_send, arrived, (p, above(direction * jump)))

    def ring_pass(place):
        for h in range(2):
            for d in (1, -1):
                if place > 0:
                    ring_copy(d, place, h).wait_recv()
                if place + 2 < LAST or h == (0 if d == 1 else 1):
                    ring_copy(d, place + 2, h).start()
        for d in (1, -1):
            ring_copy(d, place + 1, 0).start()

    def ring_leaves(group):
        blocks = pt.at[pl.ds(0, 4 + group)]
        remote(blocks, blocks, ring_send, leaf_recv.at[group], (p, z)).wait_recv()

    ring_all = remote(pt.at[pl.ds(0, NZ - 1)], pt.at[pl.ds(0, NZ - 1)], ring_send, leaf_recv.at[0], (p, z))

    def a_copy(target, part):
        return remote(piece.at[part], piece_in.at[z], a_send, a_recv, (target, z))

    def lead_copy(target, t_chip, t_core):
        src = rows.at[pl.ds(t_chip * 16, 16), pl.ds(t_core * HALF, HALF)]
        return remote(src, lead_in, lead_send, lead_recv, (target, z))

    def rs_copy(o):
        t_chip = wrapped(chip + o, CHIPS)
        return remote(masked.at[2, pl.ds(pl.multiple_of(t_chip * 16, 16), 16)], landed.at[o], rs_send, rs_recv, (near(o), z))

    def ag_copy(o):
        return remote(mine, gathered.at[core, chip], ag_send, ag_recv, (near(o), z))

    def b_copy(o):
        return remote(piece_in.at[z], piece_in.at[z], b_send, b_recv, (p, above(o)))

    sib_p = remote(masked.at[1 - core], from_sibling, p_send, p_recv, (sibling, z))
    sib_g = remote(gathered.at[core], gathered.at[core], g_send, g_recv, (sibling, z))
    c_copies = [remote(wide.at[relay], wide.at[relay], c_send, c_recv, (2 * other + c, z)) for other, c in square]
    here = (p, z)
    rs_all = remote(masked.at[2, pl.ds(0, 15 * 16)], landed.at[pl.ds(1, 15)], rs_send, rs_recv, here)
    ag_all = remote(gathered.at[core, pl.ds(0, 15)], gathered.at[core, pl.ds(0, 15)], ag_send, ag_recv, here)
    c_all = remote(wide.at[pl.ds(0, 448)], wide.at[pl.ds(0, 448)], c_send, c_recv, here)
    b_all = remote(piece_in.at[pl.ds(0, 15)], piece_in.at[pl.ds(0, 15)], b_send, b_recv, here)
    lead_all = remote(rows.at[pl.ds(0, 31 * 8)], rows.at[pl.ds(0, 31 * 8)], lead_send, lead_recv, here)
    a_all = remote(masked.at[0, pl.ds(0, 124)], masked.at[0, pl.ds(0, 124)], a_send, a_recv, here)

    def a_start():
        @pl.when(is_root)
        def _():
            for t in sorted(range(1, 2 * CHIPS), key=lambda t: -(2 - abs(t // 8 - 2) - abs(t // 2 % 4 - 2))):
                a_copy(t, part_of(t)).start()
            piece_in[z] = piece[0]

    def lead_start():
        @pl.when(is_root)
        def _():
            for t in range(1, 2 * CHIPS):
                lead_copy(t, t // 2, t % 2).start()
            lead_in[...] = rows[0:16, 0:HALF]

    def b_start():
        @pl.when(p > 0)
        def _():
            a_copy(0, 0).wait_recv()
        pl.semaphore_wait(known, 2)
        for o in (8, 7, 9, 6, 10, 5, 11, 4, 12, 3, 13, 2, 14, 1, 15):
            b_copy(o).start()

    def c_start():
        b_all.wait_recv()
        for k in range(NZ):
            column[4 * k : 4 * k + 4, :] = piece_in[k]
        wide[relay, :] = column[...]
        for copy in c_copies:
            copy.start()

    def rs_start():
        sib_p.wait_recv()
        masked[2] = masked[core] + from_sibling[...]
        for o in range(1, CHIPS):
            rs_copy(o).start()

    def ag_start():
        rs_all.wait_recv()
        @pl.when(p > 0)
        def _():
            lead_copy(0, 0, 0).wait_recv()
        total = masked[2, pl.ds(chip * 16, 16)]
        for o in range(1, CHIPS):
            total = total + landed[o]
        mine[0] = total
        mine[1] = lead_in[...]
        gathered[core, chip] = mine[...]
        for o in range(1, CHIPS):
            ag_copy(o).start()

    def g_start():
        ag_all.wait_recv()
        sib_g.start()

    def swap_rows():
        sib_g.wait_recv()
        for h in range(2):
            leading[:, h * HALF : (h + 1) * HALF] = gathered[h, :, 1].reshape(NB, HALF)
        lead_high, lead_low = split(leading[...])
        ones = jnp.ones((NB, COLS), BF16)
        for n in range(ROWS // CHUNK):
            index = lax.broadcasted_iota(jnp.int32, (CHUNK, NB), 0) + (row_start + n * CHUNK)
            chosen = jnp.where(index == pivot_lanes[...], 1.0, 0.0).astype(BF16)
            replaced = dot1(chosen, lead_high) + dot1(chosen, lead_low)
            part = slice(n * CHUNK, (n + 1) * CHUNK)
            rows[part, :] = jnp.where(dot1(chosen, ones) > 0.5, replaced, rows[part, :])

    def split_blocks(*places):
        for place in places:
            block = above(place)
            high, low = split(pt[block])
            part = pl.ds(pl.multiple_of(WIDTH * block, WIDTH), WIDTH)
            panel_high[part, :] = high
            panel_low[part, :] = low

    a_start()
    ring_pass(0)
    pivot_copy.wait()
    lanes_copy.wait()
    slab_copy.wait()

    row_start = p * ROWS

    def pick(k, carry):
        local = piv[k] - row_start
        held = (local >= 0) & (local < ROWS)
        row = rows[pl.ds(jnp.clip(local, 0, ROWS - 1), 1), :]
        row = jnp.where(held, row, 0.0)
        masked[0, pl.ds(k, 1), :] = row[:, :HALF]
        masked[1, pl.ds(k, 1), :] = row[:, HALF:]
        return carry

    lax.fori_loop(0, NB, pick, 0, unroll=8)

    sib_p.start()
    lead_start()
    rs_start()
    b_start()
    ring_pass(2)
    split_blocks(0, 2, -2)
    ag_start()
    ring_pass(4)
    split_blocks(4, -4)
    c_start()
    ring_pass(6)
    g_start()
    ring_leaves(0)
    split_blocks(1, -1, 3, -3, 6, -6)
    @pl.when(is_root)
    def _():
        lead_all.wait_send()
    swap_rows()
    c_all.wait_recv()

    for h in range(2):
        for g in range(4):
            upper_t[pl.ds(h * NB + g, 64, stride=4), :] = wide[h * NB + 64 * g : h * NB + 64 * g + 64, :]
    corner = split(upper_t[NB : NB + HALF, :].T)
    top = split(invert(upper_t[0:HALF, :].T))
    bottom = split(invert(upper_t[NB + HALF : 2 * NB, :].T))

    def pivot_half(h):
        return jnp.concatenate([gathered[c, 8 * h : 8 * h + 8, 0].reshape(HALF, HALF) for c in range(2)], axis=1)

    upper_first = dot3(top, split(pivot_half(0)))
    upper_second = dot3(bottom, split(pivot_half(1) - dot3(corner, split(upper_first))))
    upper = jnp.concatenate([upper_first, upper_second], axis=0)
    upper_parts = split(upper)

    ring_leaves(1)
    split_blocks(5, -5, 7, -7, 8)

    for n in range(ROWS // CHUNK):
        part = slice(n * CHUNK, (n + 1) * CHUNK)
        value = rows[part, :] - dot3((panel_high[:, part], panel_low[:, part]), upper_parts, 0)
        if n == 0:
            value = jnp.where(is_root, upper, value)
        out[part, :] = value

    for copy in (sib_p, sib_g, rs_all, ag_all, b_all, c_all, ring_all):
        copy.wait_send()
    @pl.when(is_root)
    def _():
        a_all.wait_send()


def split(a):
    high = a.astype(BF16)
    return high, (a - high.astype(F32)).astype(BF16)


def dot1(a, b, dim=1):
    return lax.dot_general(a, b, (((dim,), (0,)), ((), ())), preferred_element_type=F32)


def dot3(a, b, dim=1):
    return dot1(a[0], b[0], dim) + (dot1(a[0], b[1], dim) + dot1(a[1], b[0], dim))


def invert(square):
    row = lax.broadcasted_iota(jnp.int32, (HALF, HALF), 0)
    col = lax.broadcasted_iota(jnp.int32, (HALF, HALF), 1)
    lower = jnp.where(row > col, square, 0.0)
    blocks = HALF // BASE
    on_diag = (row // BASE) == (col // BASE)
    packed = jnp.sum(jnp.where(on_diag, lower, 0.0).reshape(blocks, BASE, HALF), axis=0)
    small_row = lax.broadcasted_iota(jnp.int32, (BASE, HALF), 0)
    small_col = lax.broadcasted_iota(jnp.int32, (BASE, HALF), 1)
    inverse = jnp.where(small_row == small_col % BASE, 1.0, 0.0)
    for k in range(BASE - 1):
        factor = jnp.take_along_axis(packed, (small_col // BASE) * BASE + k, axis=1)
        inverse = inverse - factor * inverse[k : k + 1, :]
    inverse = jnp.where(on_diag, jnp.concatenate([inverse] * blocks, axis=0), 0.0)
    size = BASE
    while size < HALF:
        same = (row // (2 * size)) == (col // (2 * size))
        below = same & ((row // size) % 2 == 1) & ((col // size) % 2 == 0)
        parts = split(inverse)
        inverse = inverse - dot3(parts, split(dot3(split(jnp.where(below, lower, 0.0)), parts)))
        size *= 2
    return inverse


def local(slab, panel, pivots):
    dma = pltpu.SemaphoreType.DMA
    hbm = pl.BlockSpec(memory_space=pltpu.HBM)
    return pl.pallas_call(
        exchange_kernel,
        name="exchange",
        out_shape=jax.ShapeDtypeStruct((ROWS, COLS), F32),
        in_specs=[hbm] * 4,
        out_specs=pl.BlockSpec(memory_space=pltpu.VMEM),
        scratch_shapes=[
            pltpu.VMEM((NZ, WIDTH, ROWS), F32),
            pltpu.VMEM((2, CHIPS, 2, 16, HALF), F32),
            pltpu.VMEM((2 * NB, HALF), F32),
            pltpu.SMEM((NB,), jnp.int32),
            pltpu.VMEM((1, NB), jnp.int32),
            pltpu.VMEM((2 * NB, HALF), F32),
            pltpu.VMEM((NB, COLS), F32),
            pltpu.VMEM((NB, ROWS), BF16),
            pltpu.VMEM((NB, ROWS), BF16),
            pltpu.VMEM((ROWS, COLS), F32),
            pltpu.VMEM((3, NB, HALF), F32),
            pltpu.VMEM((NB, HALF), F32),
            pltpu.VMEM((CHIPS, 16, HALF), F32),
            pltpu.VMEM((2, 16, HALF), F32),
            pltpu.VMEM((16, HALF), F32),
            pltpu.VMEM((8, 4, HALF), F32),
            pltpu.VMEM((NZ, 4, HALF), F32),
            pltpu.VMEM((4 * NZ, HALF), F32),
            dma((4,)),
            dma, dma((2, 3, 2)), dma((2,)),
            dma, dma,
            dma, dma,
            dma, dma,
            dma, dma,
            dma, dma,
            dma, dma,
            dma, dma,
            dma, dma,
            pltpu.SemaphoreType.REGULAR,
        ],
        compiler_params=pltpu.CompilerParams(
            collective_id=0, has_side_effects=True, vmem_limit_bytes=24576 * 1024
        ),
    )(*(pltpu.with_memory_space_constraint(a, pltpu.HBM) for a in (pivots, pivots.reshape(1, NB), slab, panel.T)))


def solution(mesh):
    return jax.shard_map(
        local,
        mesh=mesh,
        in_specs=(P("prow", "pcol"), P("prow", "pcol"), P()),
        out_specs=P("prow", "pcol"),
        check_vma=False,
    )
```

```python
import jax
import jax.numpy as jnp
from jax import lax
from jax.experimental import pallas as pl
from jax.experimental.pallas import tpu as pltpu
from jax.sharding import PartitionSpec as P

MESH = pl.DeviceIdType.MESH
F32 = jnp.float32
BF16 = jnp.bfloat16
NB = 256
ROWS = 1024
COLS = 256
NZ = 16
CHIPS = 16
HALF = 128
WIDTH = 16
LAST = 8
CHUNK = 256
BASE = 32


def exchange_kernel(
    pivots, pivot_row, slab, panel, out,
    pt, gathered, wide, piv, pivot_lanes, upper_t, leading, panel_high, panel_low, rows, masked, from_sibling, landed, mine, lead_in, lead_rows, piece, piece_in, column,
    local_sem, ring_send, ring_recv, leaf_recv, x_send, x_recv, a_send, a_recv, b_send, b_recv, c_send, c_recv,
    lead_x_send, lead_x_recv, lead_send, lead_recv, p_send, p_recv, rs_send, rs_recv, ag_send, ag_recv, g_send, g_recv, line_known, near_known, far_known,
):
    p = lax.axis_index("prow")
    z = lax.axis_index("pcol")
    chip = lax.div(p, 2)
    core = lax.rem(p, 2)
    sibling = 2 * chip + 1 - core
    is_root = p == 0
    relays = lax.rem(p, 8) == 0

    def wrapped(index, size):
        return jnp.where(index >= size, index - size, jnp.where(index < 0, index + size, index))

    nears = [2 * wrapped(chip + o, CHIPS) + core for o in range(CHIPS)]
    aboves = [wrapped(z + o, NZ) if o < 9 else wrapped(z + o - NZ, NZ) for o in range(NZ)]

    def near(o):
        return nears[o]

    def above(o):
        return aboves[o % NZ]

    x, y = lax.div(chip, 4), lax.rem(chip, 4)
    x_odd, y_odd = lax.rem(x, 2), lax.rem(y, 2)
    across, along = 4 - 8 * x_odd, 1 - 2 * y_odd
    square = [(chip + move, c) for move in (across + along, across, along) for c in (core, 1 - core)]
    square.append((chip, 1 - core))
    lines = [2 * wrapped(chip + 4 * o, CHIPS) + core for o in (2, 1, 3)]
    lines_y = [8 * x + 2 * jnp.where(y + o >= 4, y + o - 4, y + o) + core for o in (2, 1, 3)]

    mine_part = 2 * x_odd + y_odd
    relay = pl.ds(pl.multiple_of(core * NB + 64 * mine_part, 64), 64)

    barrier = pltpu.get_barrier_semaphore()

    def greet(device):
        pl.semaphore_signal(barrier, inc=1, device_id=device, device_id_type=MESH)

    pivot_copy = pltpu.make_async_copy(pivots, piv, local_sem.at[2])
    panel_copy = pltpu.make_async_copy(panel, pt.at[z], local_sem.at[0])
    slab_copy = pltpu.make_async_copy(slab, rows, local_sem.at[1])
    lanes_copy = pltpu.make_async_copy(pivot_row, pivot_lanes, local_sem.at[3])
    panel_copy.start()
    slab_copy.start()
    pivot_copy.start()
    lanes_copy.start()

    for o in (2, 1):
        greet((p, above(o)))
        greet((p, above(-o)))
    for device in lines + lines_y:
        greet((device, z))
    for other, c in square[1::2]:
        greet((2 * other + c, z))
    greet((sibling, z))

    @pl.when(relays)
    def _():
        for j in range(1, 4):
            greet((8 * x + 2 * j + 1, z))

    relayed_by_other = (core == 1) & (y > 0)

    @pl.when(relayed_by_other)
    def _():
        greet((8 * x, z))

    panel_copy.wait()

    @pl.when(is_root)
    def _():
        for k in range(WIDTH):
            for h in range(2):
                piece[2 * (k % 4) + h, k // 4 : k // 4 + 1, :] = pt[z, k : k + 1, h * HALF : (h + 1) * HALF]

    greeted = 4 + 6 + 3 + 1
    pl.semaphore_wait(barrier, greeted + jnp.where(relays, 3, jnp.where(relayed_by_other, 1, 0)))

    for device in lines:
        pl.semaphore_signal(line_known, inc=1, device_id=(device, z), device_id_type=MESH)
    for o in (2, -2):
        pl.semaphore_signal(near_known, inc=1, device_id=(p, above(o)), device_id_type=MESH)

    def remote(src, dst, send, recv, device):
        return pltpu.make_async_remote_copy(
            src_ref=src, dst_ref=dst, send_sem=send, recv_sem=recv, device_id=device, device_id_type=MESH
        )

    def ring_copy(direction, place, half):
        jump = 2 - place % 2
        block = above(-direction * (place - jump))
        d = (direction + 1) // 2
        if place % 2:
            part, arrived = pt.at[block], leaf_recv.at[place // 4]
        else:
            part = pt.at[block, pl.ds(8 * half, 8)]
            arrived = leaf_recv.at[1] if place == LAST else ring_recv.at[d, place // 2 - 1, half]
        return remote(part, part, ring_send, arrived, (p, above(direction * jump)))

    def ring_pass(place):
        for h in range(2):
            for d in (1, -1):
                if place > 0:
                    ring_copy(d, place, h).wait_recv()
                if place + 2 < LAST or h == (0 if d == 1 else 1):
                    ring_copy(d, place + 2, h).start()
        for d in (1, -1):
            ring_copy(d, place + 1, 0).start()

    def ring_leaves(group):
        blocks = pt.at[pl.ds(0, 4 + group)]
        remote(blocks, blocks, ring_send, leaf_recv.at[group], (p, z)).wait_recv()

    ring_all = remote(pt.at[pl.ds(0, NZ - 1)], pt.at[pl.ds(0, NZ - 1)], ring_send, leaf_recv.at[0], (p, z))

    mine_first = pl.multiple_of(4 * x_odd, 4)

    def x_copy(line):
        return remote(piece.at[pl.ds(4 * (line % 2), 4)], piece.at[pl.ds(4 * (line % 2), 4)], x_send, x_recv, (8 * line, z))

    def a_copy(target, j, c):
        return remote(piece.at[mine_first + 2 * (j % 2) + c], piece_in.at[z], a_send, a_recv, (target, z))

    def lead_x_copy(line):
        return remote(rows.at[pl.ds(64 * line, 64)], lead_rows, lead_x_send, lead_x_recv, (8 * line, z))

    def lead_copy(target, j, c):
        src = lead_rows.at[pl.ds(16 * j, 16), pl.ds(c * HALF, HALF)]
        return remote(src, lead_in, lead_send, lead_recv, (target, z))

    targets = [(8 * x + 2 * j + c, j, c) for j in (2, 1, 3) for c in range(2)] + [(8 * x + 1, 0, 1)]

    def rs_copy(o):
        t_chip = wrapped(chip + o, CHIPS)
        return remote(masked.at[2, pl.ds(pl.multiple_of(t_chip * 16, 16), 16)], landed.at[o], rs_send, rs_recv, (near(o), z))

    def ag_copy(o):
        return remote(mine, gathered.at[core, chip], ag_send, ag_recv, (near(o), z))

    def b_copy(o):
        return remote(piece_in.at[z], piece_in.at[z], b_send, b_recv, (p, above(o)))

    sib_p = remote(masked.at[1 - core], from_sibling, p_send, p_recv, (sibling, z))
    sib_g = remote(gathered.at[core], gathered.at[core], g_send, g_recv, (sibling, z))
    c_copies = [remote(wide.at[relay], wide.at[relay], c_send, c_recv, (2 * other + c, z)) for other, c in square]
    here = (p, z)
    rs_all = remote(masked.at[2, pl.ds(0, 15 * 16)], landed.at[pl.ds(1, 15)], rs_send, rs_recv, here)
    ag_all = remote(gathered.at[core, pl.ds(0, 15)], gathered.at[core, pl.ds(0, 15)], ag_send, ag_recv, here)
    c_all = remote(wide.at[pl.ds(0, 448)], wide.at[pl.ds(0, 448)], c_send, c_recv, here)
    b_all = remote(piece_in.at[pl.ds(0, 15)], piece_in.at[pl.ds(0, 15)], b_send, b_recv, here)
    x_all = remote(masked.at[0, pl.ds(0, 48)], masked.at[0, pl.ds(0, 48)], x_send, x_recv, here)
    a_all = remote(masked.at[0, pl.ds(0, 28)], masked.at[0, pl.ds(0, 28)], a_send, a_recv, here)
    lead_x_all = remote(rows.at[pl.ds(0, 192)], rows.at[pl.ds(0, 192)], lead_x_send, lead_x_recv, here)
    lead_all = remote(masked.at[0, pl.ds(0, 112)], masked.at[0, pl.ds(0, 112)], lead_send, lead_recv, here)

    def x_start():
        @pl.when(is_root)
        def _():
            for line in (2, 1, 3):
                x_copy(line).start()

    def lead_x_start():
        @pl.when(is_root)
        def _():
            for line in (2, 1, 3):
                lead_x_copy(line).start()
            lead_rows[...] = rows[0:64, :]

    def a_start():
        @pl.when(relays)
        def _():
            @pl.when(p > 0)
            def _():
                x_copy(0).wait_recv()
            for target in targets:
                a_copy(*target).start()
            piece_in[z] = piece[mine_first]

    def lead_start():
        @pl.when(relays)
        def _():
            @pl.when(p > 0)
            def _():
                lead_x_copy(0).wait_recv()
            for target in targets:
                lead_copy(*target).start()
            lead_in[...] = lead_rows[0:16, 0:HALF]

    def tell_column():
        pl.semaphore_wait(near_known, 2)
        for o in (4, -4):
            pl.semaphore_signal(far_known, inc=1, device_id=(p, above(o)), device_id_type=MESH)

    def b_start():
        @pl.when(jnp.logical_not(relays))
        def _():
            a_copy(0, 0, 0).wait_recv()
        for o in (4, 12, 3, 13, 2, 14, 1, 15):
            b_copy(o).start()

    def b_far_start():
        pl.semaphore_wait(far_known, 2)
        for o in (8, 7, 9, 6, 10, 5, 11):
            b_copy(o).start()

    def c_start():
        b_all.wait_recv()
        for k in range(NZ):
            column[4 * k : 4 * k + 4, :] = piece_in[k]
        wide[relay, :] = column[...]
        for copy in c_copies:
            copy.start()

    def rs_start():
        sib_p.wait_recv()
        masked[2] = masked[core] + from_sibling[...]
        pl.semaphore_wait(line_known, 3)
        for o in range(1, CHIPS):
            rs_copy(o).start()

    def ag_start():
        rs_all.wait_recv()
        @pl.when(jnp.logical_not(relays))
        def _():
            lead_copy(0, 0, 0).wait_recv()
        total = masked[2, pl.ds(chip * 16, 16)]
        for o in range(1, CHIPS):
            total = total + landed[o]
        mine[0] = total
        mine[1] = lead_in[...]
        gathered[core, chip] = mine[...]
        for o in range(1, CHIPS):
            ag_copy(o).start()

    def g_start():
        ag_all.wait_recv()
        sib_g.start()

    def swap_rows():
        sib_g.wait_recv()
        for h in range(2):
            leading[:, h * HALF : (h + 1) * HALF] = gathered[h, :, 1].reshape(NB, HALF)
        lead_high, lead_low = split(leading[...])
        ones = jnp.ones((NB, COLS), BF16)
        for n in range(ROWS // CHUNK):
            index = lax.broadcasted_iota(jnp.int32, (CHUNK, NB), 0) + (row_start + n * CHUNK)
            chosen = jnp.where(index == pivot_lanes[...], 1.0, 0.0).astype(BF16)
            replaced = dot1(chosen, lead_high) + dot1(chosen, lead_low)
            part = slice(n * CHUNK, (n + 1) * CHUNK)
            rows[part, :] = jnp.where(dot1(chosen, ones) > 0.5, replaced, rows[part, :])

    def split_blocks(*places):
        for place in places:
            block = above(place)
            high, low = split(pt[block])
            part = pl.ds(pl.multiple_of(WIDTH * block, WIDTH), WIDTH)
            panel_high[part, :] = high
            panel_low[part, :] = low

    x_start()
    ring_pass(0)
    pivot_copy.wait()
    lanes_copy.wait()
    slab_copy.wait()

    row_start = p * ROWS

    def pick(k, carry):
        local = piv[k] - row_start
        held = (local >= 0) & (local < ROWS)
        row = rows[pl.ds(jnp.clip(local, 0, ROWS - 1), 1), :]
        row = jnp.where(held, row, 0.0)
        masked[0, pl.ds(k, 1), :] = row[:, :HALF]
        masked[1, pl.ds(k, 1), :] = row[:, HALF:]
        return carry

    lax.fori_loop(0, NB, pick, 0, unroll=8)

    sib_p.start()
    lead_x_start()
    a_start()
    tell_column()
    rs_start()
    lead_start()
    ring_pass(2)
    b_start()
    split_blocks(0, 2, -2)
    b_far_start()
    ag_start()
    ring_pass(4)
    split_blocks(4, -4)
    ring_leaves(0)
    split_blocks(1, -1, 3, -3)
    ring_pass(6)
    c_start()
    g_start()
    split_blocks(6, -6)
    @pl.when(is_root)
    def _():
        lead_x_all.wait_send()
    swap_rows()
    c_all.wait_recv()

    for h in range(2):
        for g in range(4):
            upper_t[pl.ds(h * NB + g, 64, stride=4), :] = wide[h * NB + 64 * g : h * NB + 64 * g + 64, :]
    corner = split(upper_t[NB : NB + HALF, :].T)
    top = split(invert(upper_t[0:HALF, :].T))
    bottom = split(invert(upper_t[NB + HALF : 2 * NB, :].T))

    def pivot_half(h):
        return jnp.concatenate([gathered[c, 8 * h : 8 * h + 8, 0].reshape(HALF, HALF) for c in range(2)], axis=1)

    upper_first = dot3(top, split(pivot_half(0)))
    upper_second = dot3(bottom, split(pivot_half(1) - dot3(corner, split(upper_first))))
    upper = jnp.concatenate([upper_first, upper_second], axis=0)
    upper_parts = split(upper)

    ring_leaves(1)
    split_blocks(5, -5, 7, -7, 8)

    for n in range(ROWS // CHUNK):
        part = slice(n * CHUNK, (n + 1) * CHUNK)
        value = rows[part, :] - dot3((panel_high[:, part], panel_low[:, part]), upper_parts, 0)
        if n == 0:
            value = jnp.where(is_root, upper, value)
        out[part, :] = value

    for copy in (sib_p, sib_g, rs_all, ag_all, b_all, c_all, ring_all):
        copy.wait_send()
    @pl.when(relays)
    def _():
        a_all.wait_send()
        lead_all.wait_send()

    @pl.when(is_root)
    def _():
        x_all.wait_send()


def split(a):
    high = a.astype(BF16)
    return high, (a - high.astype(F32)).astype(BF16)


def dot1(a, b, dim=1):
    return lax.dot_general(a, b, (((dim,), (0,)), ((), ())), preferred_element_type=F32)


def dot3(a, b, dim=1):
    return dot1(a[0], b[0], dim) + (dot1(a[0], b[1], dim) + dot1(a[1], b[0], dim))


def invert(square):
    row = lax.broadcasted_iota(jnp.int32, (HALF, HALF), 0)
    col = lax.broadcasted_iota(jnp.int32, (HALF, HALF), 1)
    lower = jnp.where(row > col, square, 0.0)
    blocks = HALF // BASE
    on_diag = (row // BASE) == (col // BASE)
    packed = jnp.sum(jnp.where(on_diag, lower, 0.0).reshape(blocks, BASE, HALF), axis=0)
    small_row = lax.broadcasted_iota(jnp.int32, (BASE, HALF), 0)
    small_col = lax.broadcasted_iota(jnp.int32, (BASE, HALF), 1)
    inverse = jnp.where(small_row == small_col % BASE, 1.0, 0.0)
    for k in range(BASE - 1):
        factor = jnp.take_along_axis(packed, (small_col // BASE) * BASE + k, axis=1)
        inverse = inverse - factor * inverse[k : k + 1, :]
    inverse = jnp.where(on_diag, jnp.concatenate([inverse] * blocks, axis=0), 0.0)
    size = BASE
    while size < HALF:
        same = (row // (2 * size)) == (col // (2 * size))
        below = same & ((row // size) % 2 == 1) & ((col // size) % 2 == 0)
        parts = split(inverse)
        inverse = inverse - dot3(parts, split(dot3(split(jnp.where(below, lower, 0.0)), parts)))
        size *= 2
    return inverse


def local(slab, panel, pivots):
    dma = pltpu.SemaphoreType.DMA
    hbm = pl.BlockSpec(memory_space=pltpu.HBM)
    return pl.pallas_call(
        exchange_kernel,
        name="exchange",
        out_shape=jax.ShapeDtypeStruct((ROWS, COLS), F32),
        in_specs=[hbm] * 4,
        out_specs=pl.BlockSpec(memory_space=pltpu.VMEM),
        scratch_shapes=[
            pltpu.VMEM((NZ, WIDTH, ROWS), F32),
            pltpu.VMEM((2, CHIPS, 2, 16, HALF), F32),
            pltpu.VMEM((2 * NB, HALF), F32),
            pltpu.SMEM((NB,), jnp.int32),
            pltpu.VMEM((1, NB), jnp.int32),
            pltpu.VMEM((2 * NB, HALF), F32),
            pltpu.VMEM((NB, COLS), F32),
            pltpu.VMEM((NB, ROWS), BF16),
            pltpu.VMEM((NB, ROWS), BF16),
            pltpu.VMEM((ROWS, COLS), F32),
            pltpu.VMEM((3, NB, HALF), F32),
            pltpu.VMEM((NB, HALF), F32),
            pltpu.VMEM((CHIPS, 16, HALF), F32),
            pltpu.VMEM((2, 16, HALF), F32),
            pltpu.VMEM((16, HALF), F32),
            pltpu.VMEM((64, COLS), F32),
            pltpu.VMEM((8, 4, HALF), F32),
            pltpu.VMEM((NZ, 4, HALF), F32),
            pltpu.VMEM((4 * NZ, HALF), F32),
            dma((4,)),
            dma, dma((2, 3, 2)), dma((2,)),
            dma, dma,
            dma, dma,
            dma, dma,
            dma, dma,
            dma, dma,
            dma, dma,
            dma, dma,
            dma, dma,
            dma, dma,
            dma, dma,
            pltpu.SemaphoreType.REGULAR,
            pltpu.SemaphoreType.REGULAR,
            pltpu.SemaphoreType.REGULAR,
        ],
        compiler_params=pltpu.CompilerParams(
            collective_id=0, has_side_effects=True, vmem_limit_bytes=24576 * 1024
        ),
    )(*(pltpu.with_memory_space_constraint(a, pltpu.HBM) for a in (pivots, pivots.reshape(1, NB), slab, panel.T)))


def solution(mesh):
    return jax.shard_map(
        local,
        mesh=mesh,
        in_specs=(P("prow", "pcol"), P("prow", "pcol"), P()),
        out_specs=P("prow", "pcol"),
        check_vma=False,
    )
```

```python
import jax
import jax.numpy as jnp
from jax import lax
from jax.experimental import pallas as pl
from jax.experimental.pallas import tpu as pltpu
from jax.sharding import PartitionSpec as P

MESH = pl.DeviceIdType.MESH
F32 = jnp.float32
BF16 = jnp.bfloat16
NB = 256
ROWS = 1024
COLS = 256
NZ = 16
CHIPS = 16
HALF = 128
WIDTH = 16
LAST = 8
PARTS = 4
LEAVES_AFTER = {0: (1,), 2: (3,), 4: (5,), 6: (7,)}
REACH = 4
CHUNK = 256
BASE = 32


def exchange_kernel(
    pivots, pivot_row, slab, panel, out,
    pt, gathered, wide, piv, pivot_lanes, upper_t, leading, panel_high, panel_low, rows, masked, from_sibling, landed, mine, lead_in, piece, piece_in, column,
    local_sem, ring_send, ring_recv, leaf_recv, a_send, a_recv, b_send, b_recv, c_send, c_recv,
    lead_send, lead_recv, p_send, p_recv, rs_send, rs_recv, ag_send, ag_recv, g_send, g_recv, known,
):
    p = lax.axis_index("prow")
    z = lax.axis_index("pcol")
    chip = lax.div(p, 2)
    core = lax.rem(p, 2)
    sibling = 2 * chip + 1 - core
    is_root = p == 0
    outer = (core == 1) & (chip > 0)

    def wrapped(index, size):
        return jnp.where(index >= size, index - size, jnp.where(index < 0, index + size, index))

    nears = [2 * wrapped(chip + o, CHIPS) + core for o in range(CHIPS)]
    aboves = [wrapped(z + o, NZ) if o < 9 else wrapped(z + o - NZ, NZ) for o in range(NZ)]

    def near(o):
        return nears[o]

    def above(o):
        return aboves[o % NZ]

    x, y = lax.div(chip, 4), lax.rem(chip, 4)
    x_odd, y_odd = lax.rem(x, 2), lax.rem(y, 2)
    across, along = 4 - 8 * x_odd, 1 - 2 * y_odd
    square = [(chip + move, c) for move in (across + along, across, along) for c in (core, 1 - core)]
    square.append((chip, 1 - core))

    def part_of(target):
        return 4 * (target // 8 % 2) + 2 * (target // 2 % 2) + target % 2

    mine_part = 2 * x_odd + y_odd
    relay = pl.ds(pl.multiple_of(core * NB + 64 * mine_part, 64), 64)

    barrier = pltpu.get_barrier_semaphore()

    def greet(device):
        pl.semaphore_signal(barrier, inc=1, device_id=device, device_id_type=MESH)

    pivot_copy = pltpu.make_async_copy(pivots, piv, local_sem.at[2])
    panel_copy = pltpu.make_async_copy(panel, pt.at[z], local_sem.at[0])
    slab_copy = pltpu.make_async_copy(slab, rows, local_sem.at[1])
    lanes_copy = pltpu.make_async_copy(pivot_row, pivot_lanes, local_sem.at[3])
    panel_copy.start()
    slab_copy.start()
    pivot_copy.start()
    lanes_copy.start()

    for o in (10, 9, 11, 6, 14):
        greet((near(o), z))
    for o in range(REACH, 0, -1):
        greet((p, above(o)))
        greet((p, above(-o)))
    for o in (2, 5, 7, 8, 13, 15, 1, 3, 4, 12):
        greet((near(o), z))
    for other, c in square[1::2]:
        greet((2 * other + c, z))
    greet((sibling, z))

    @pl.when(is_root)
    def _():
        for o in range(1, CHIPS):
            greet((2 * o + 1, z))

    @pl.when(outer)
    def _():
        greet((0, z))

    panel_copy.wait()
    for k in range(WIDTH):
        for h in range(2):
            piece[2 * (k % 4) + h, k // 4 : k // 4 + 1, :] = pt[z, k : k + 1, h * HALF : (h + 1) * HALF]
    greeted = 2 * REACH + CHIPS + 3
    pl.semaphore_wait(barrier, greeted + jnp.where(is_root, CHIPS - 1, jnp.where(outer, 1, 0)))

    for o in (REACH, -REACH):
        pl.semaphore_signal(known, inc=1, device_id=(p, above(o)), device_id_type=MESH)

    def remote(src, dst, send, recv, device):
        return pltpu.make_async_remote_copy(
            src_ref=src, dst_ref=dst, send_sem=send, recv_sem=recv, device_id=device, device_id_type=MESH
        )

    def ring_copy(direction, place, piece_of):
        jump = 2 - place % 2
        block = above(-direction * (place - jump))
        d = (direction + 1) // 2
        if place % 2:
            part, arrived = pt.at[block], leaf_recv.at[place // 4]
        else:
            part = pt.at[block, pl.ds(8 * (2 * piece_of // PARTS), 8)]
            if PARTS == 1:
                part = pt.at[block]
            elif PARTS > 2:
                width = 2 * ROWS // PARTS
                part = pt.at[block, pl.ds(8 * (2 * piece_of // PARTS), 8), pl.ds(width * (piece_of % (PARTS // 2)), width)]
            arrived = leaf_recv.at[1] if place == LAST else ring_recv.at[d, place // 2 - 1, piece_of]
        return remote(part, part, ring_send, arrived, (p, above(direction * jump)))

    def ring_pass(place):
        for q in range(PARTS):
            for d in (1, -1):
                if place > 0:
                    ring_copy(d, place, q).wait_recv()
                if place + 2 < LAST or (2 * q < PARTS) == (d == 1):
                    ring_copy(d, place + 2, q).start()
        for leaf in LEAVES_AFTER[place]:
            for d in (1, -1):
                ring_copy(d, leaf, 0).start()

    def ring_leaves(group):
        blocks = pt.at[pl.ds(0, 4 + group)]
        remote(blocks, blocks, ring_send, leaf_recv.at[group], (p, z)).wait_recv()

    ring_all = remote(pt.at[pl.ds(0, NZ - 1)], pt.at[pl.ds(0, NZ - 1)], ring_send, leaf_recv.at[0], (p, z))

    def a_copy(target, part):
        return remote(piece.at[part], piece_in.at[z], a_send, a_recv, (target, z))

    def lead_copy(target, t_chip, t_core):
        src = rows.at[pl.ds(t_chip * 16, 16), pl.ds(t_core * HALF, HALF)]
        return remote(src, lead_in, lead_send, lead_recv, (target, z))

    def rs_copy(o):
        t_chip = wrapped(chip + o, CHIPS)
        return remote(masked.at[2, pl.ds(pl.multiple_of(t_chip * 16, 16), 16)], landed.at[o], rs_send, rs_recv, (near(o), z))

    def ag_copy(o):
        return remote(mine, gathered.at[core, chip], ag_send, ag_recv, (near(o), z))

    def b_copy(o):
        return remote(piece_in.at[z], piece_in.at[z], b_send, b_recv, (p, above(o)))

    sib_p = remote(masked.at[1 - core], from_sibling, p_send, p_recv, (sibling, z))
    sib_g = remote(gathered.at[core], gathered.at[core], g_send, g_recv, (sibling, z))
    c_copies = [remote(wide.at[relay], wide.at[relay], c_send, c_recv, (2 * other + c, z)) for other, c in square]
    here = (p, z)
    rs_all = remote(masked.at[2, pl.ds(0, 15 * 16)], landed.at[pl.ds(1, 15)], rs_send, rs_recv, here)
    ag_all = remote(gathered.at[core, pl.ds(0, 15)], gathered.at[core, pl.ds(0, 15)], ag_send, ag_recv, here)
    c_all = remote(wide.at[pl.ds(0, 448)], wide.at[pl.ds(0, 448)], c_send, c_recv, here)
    b_all = remote(piece_in.at[pl.ds(0, 15)], piece_in.at[pl.ds(0, 15)], b_send, b_recv, here)
    lead_all = remote(rows.at[pl.ds(0, 31 * 8)], rows.at[pl.ds(0, 31 * 8)], lead_send, lead_recv, here)
    a_all = remote(masked.at[0, pl.ds(0, 124)], masked.at[0, pl.ds(0, 124)], a_send, a_recv, here)

    def a_start():
        @pl.when(is_root)
        def _():
            for t in sorted(range(1, 2 * CHIPS), key=lambda t: -(2 - abs(t // 8 - 2) - abs(t // 2 % 4 - 2))):
                a_copy(t, part_of(t)).start()
            piece_in[z] = piece[0]

    def lead_start():
        @pl.when(is_root)
        def _():
            for t in range(1, 2 * CHIPS):
                lead_copy(t, t // 2, t % 2).start()
            lead_in[...] = rows[0:16, 0:HALF]

    def b_start():
        @pl.when(p > 0)
        def _():
            a_copy(0, 0).wait_recv()
        pl.semaphore_wait(known, 2)
        for o in (8, 7, 9, 6, 10, 5, 11, 4, 12, 3, 13, 2, 14, 1, 15):
            b_copy(o).start()

    def c_start():
        b_all.wait_recv()
        for k in range(NZ):
            column[4 * k : 4 * k + 4, :] = piece_in[k]
        wide[relay, :] = column[...]
        for copy in c_copies:
            copy.start()

    def rs_start():
        sib_p.wait_recv()
        masked[2] = masked[core] + from_sibling[...]
        for o in range(1, CHIPS):
            rs_copy(o).start()

    def ag_start():
        rs_all.wait_recv()
        @pl.when(p > 0)
        def _():
            lead_copy(0, 0, 0).wait_recv()
        total = masked[2, pl.ds(chip * 16, 16)]
        for o in range(1, CHIPS):
            total = total + landed[o]
        mine[0] = total
        mine[1] = lead_in[...]
        gathered[core, chip] = mine[...]
        for o in range(1, CHIPS):
            ag_copy(o).start()

    def g_start():
        ag_all.wait_recv()
        sib_g.start()

    def swap_rows():
        for h in range(2):
            leading[:, h * HALF : (h + 1) * HALF] = gathered[h, :, 1].reshape(NB, HALF)
        lead_high, lead_low = split(leading[...])
        ones = jnp.ones((NB, COLS), BF16)
        for n in range(ROWS // CHUNK):
            index = lax.broadcasted_iota(jnp.int32, (CHUNK, NB), 0) + (row_start + n * CHUNK)
            chosen = jnp.where(index == pivot_lanes[...], 1.0, 0.0).astype(BF16)
            replaced = dot1(chosen, lead_high) + dot1(chosen, lead_low)
            part = slice(n * CHUNK, (n + 1) * CHUNK)
            rows[part, :] = jnp.where(dot1(chosen, ones) > 0.5, replaced, rows[part, :])

    def split_blocks(*places):
        for place in places:
            block = above(place)
            high, low = split(pt[block])
            part = pl.ds(pl.multiple_of(WIDTH * block, WIDTH), WIDTH)
            panel_high[part, :] = high
            panel_low[part, :] = low

    a_start()
    ring_pass(0)
    pivot_copy.wait()
    lanes_copy.wait()
    slab_copy.wait()

    row_start = p * ROWS

    def pick(k, carry):
        local = piv[k] - row_start
        held = (local >= 0) & (local < ROWS)
        row = rows[pl.ds(jnp.clip(local, 0, ROWS - 1), 1), :]
        row = jnp.where(held, row, 0.0)
        masked[0, pl.ds(k, 1), :] = row[:, :HALF]
        masked[1, pl.ds(k, 1), :] = row[:, HALF:]
        return carry

    lax.fori_loop(0, NB, pick, 0, unroll=8)

    sib_p.start()
    lead_start()
    rs_start()
    b_start()
    ring_pass(2)
    split_blocks(0, 2, -2)
    ag_start()
    ring_pass(4)
    split_blocks(4, -4)
    c_start()
    ring_pass(6)
    g_start()
    ring_leaves(0)
    split_blocks(1, -1, 3, -3, 6, -6)
    @pl.when(is_root)
    def _():
        lead_all.wait_send()
    c_all.wait_recv()

    for h in range(2):
        for g in range(4):
            upper_t[pl.ds(h * NB + g, 64, stride=4), :] = wide[h * NB + 64 * g : h * NB + 64 * g + 64, :]
    corner = split(upper_t[NB : NB + HALF, :].T)
    top = split(invert(upper_t[0:HALF, :].T))
    bottom = split(invert(upper_t[NB + HALF : 2 * NB, :].T))

    def pivot_half(h):
        return jnp.concatenate([gathered[c, 8 * h : 8 * h + 8, 0].reshape(HALF, HALF) for c in range(2)], axis=1)

    sib_g.wait_recv()
    upper_first = dot3(top, split(pivot_half(0)))
    upper_second = dot3(bottom, split(pivot_half(1) - dot3(corner, split(upper_first))))
    upper = jnp.concatenate([upper_first, upper_second], axis=0)
    upper_parts = split(upper)
    swap_rows()

    ring_leaves(1)
    split_blocks(5, -5, 7, -7, 8)

    for n in range(ROWS // CHUNK):
        part = slice(n * CHUNK, (n + 1) * CHUNK)
        value = rows[part, :] - dot3((panel_high[:, part], panel_low[:, part]), upper_parts, 0)
        if n == 0:
            value = jnp.where(is_root, upper, value)
        out[part, :] = value

    for copy in (sib_p, sib_g, rs_all, ag_all, b_all, c_all, ring_all):
        copy.wait_send()
    @pl.when(is_root)
    def _():
        a_all.wait_send()


def split(a):
    high = a.astype(BF16)
    return high, (a - high.astype(F32)).astype(BF16)


def dot1(a, b, dim=1):
    return lax.dot_general(a, b, (((dim,), (0,)), ((), ())), preferred_element_type=F32)


def dot3(a, b, dim=1):
    return dot1(a[0], b[0], dim) + (dot1(a[0], b[1], dim) + dot1(a[1], b[0], dim))


def invert(square):
    row = lax.broadcasted_iota(jnp.int32, (HALF, HALF), 0)
    col = lax.broadcasted_iota(jnp.int32, (HALF, HALF), 1)
    lower = jnp.where(row > col, square, 0.0)
    blocks = HALF // BASE
    on_diag = (row // BASE) == (col // BASE)
    packed = jnp.sum(jnp.where(on_diag, lower, 0.0).reshape(blocks, BASE, HALF), axis=0)
    small_row = lax.broadcasted_iota(jnp.int32, (BASE, HALF), 0)
    small_col = lax.broadcasted_iota(jnp.int32, (BASE, HALF), 1)
    inverse = jnp.where(small_row == small_col % BASE, 1.0, 0.0)
    for k in range(BASE - 1):
        factor = jnp.take_along_axis(packed, (small_col // BASE) * BASE + k, axis=1)
        inverse = inverse - factor * inverse[k : k + 1, :]
    inverse = jnp.where(on_diag, jnp.concatenate([inverse] * blocks, axis=0), 0.0)
    size = BASE
    while size < HALF:
        same = (row // (2 * size)) == (col // (2 * size))
        below = same & ((row // size) % 2 == 1) & ((col // size) % 2 == 0)
        parts = split(inverse)
        inverse = inverse - dot3(parts, split(dot3(split(jnp.where(below, lower, 0.0)), parts)))
        size *= 2
    return inverse


def local(slab, panel, pivots):
    dma = pltpu.SemaphoreType.DMA
    hbm = pl.BlockSpec(memory_space=pltpu.HBM)
    return pl.pallas_call(
        exchange_kernel,
        name="exchange",
        out_shape=jax.ShapeDtypeStruct((ROWS, COLS), F32),
        in_specs=[hbm] * 4,
        out_specs=pl.BlockSpec(memory_space=pltpu.VMEM),
        scratch_shapes=[
            pltpu.VMEM((NZ, WIDTH, ROWS), F32),
            pltpu.VMEM((2, CHIPS, 2, 16, HALF), F32),
            pltpu.VMEM((2 * NB, HALF), F32),
            pltpu.SMEM((NB,), jnp.int32),
            pltpu.VMEM((1, NB), jnp.int32),
            pltpu.VMEM((2 * NB, HALF), F32),
            pltpu.VMEM((NB, COLS), F32),
            pltpu.VMEM((NB, ROWS), BF16),
            pltpu.VMEM((NB, ROWS), BF16),
            pltpu.VMEM((ROWS, COLS), F32),
            pltpu.VMEM((3, NB, HALF), F32),
            pltpu.VMEM((NB, HALF), F32),
            pltpu.VMEM((CHIPS, 16, HALF), F32),
            pltpu.VMEM((2, 16, HALF), F32),
            pltpu.VMEM((16, HALF), F32),
            pltpu.VMEM((8, 4, HALF), F32),
            pltpu.VMEM((NZ, 4, HALF), F32),
            pltpu.VMEM((4 * NZ, HALF), F32),
            dma((4,)),
            dma, dma((2, 3, 4)), dma((2,)),
            dma, dma,
            dma, dma,
            dma, dma,
            dma, dma,
            dma, dma,
            dma, dma,
            dma, dma,
            dma, dma,
            pltpu.SemaphoreType.REGULAR,
        ],
        compiler_params=pltpu.CompilerParams(
            collective_id=0, has_side_effects=True, vmem_limit_bytes=24576 * 1024
        ),
    )(*(pltpu.with_memory_space_constraint(a, pltpu.HBM) for a in (pivots, pivots.reshape(1, NB), slab, panel.T)))


def solution(mesh):
    return jax.shard_map(
        local,
        mesh=mesh,
        in_specs=(P("prow", "pcol"), P("prow", "pcol"), P()),
        out_specs=P("prow", "pcol"),
        check_vma=False,
    )
```

```python
import jax
import jax.numpy as jnp
from jax import lax
from jax.experimental import pallas as pl
from jax.experimental.pallas import tpu as pltpu
from jax.sharding import PartitionSpec as P

MESH = pl.DeviceIdType.MESH
F32 = jnp.float32
BF16 = jnp.bfloat16
NB = 256
ROWS = 1024
COLS = 256
NZ = 16
CHIPS = 16
HALF = 128
WIDTH = 16
LAST = 8
LATE = (5, -5, 7, -7, 8)
PARTS = 4
LEAVES_AFTER = {0: (1,), 2: (3,), 4: (5,), 6: (7,)}
REACH = 4
CHUNK = 256
BASE = 32


def exchange_kernel(
    pivots, pivot_row, slab, panel, out,
    pt, gathered, wide, piv, pivot_lanes, upper_t, leading, panel_high, panel_low, upper_high, upper_low, late_panel, late_upper, rows, masked, from_sibling, landed, mine, lead_in, piece, piece_in, column,
    local_sem, ring_send, ring_recv, leaf_recv, a_send, a_recv, b_send, b_recv, c_send, c_recv,
    lead_send, lead_recv, p_send, p_recv, rs_send, rs_recv, ag_send, ag_recv, g_send, g_recv, known,
):
    p = lax.axis_index("prow")
    z = lax.axis_index("pcol")
    chip = lax.div(p, 2)
    core = lax.rem(p, 2)
    sibling = 2 * chip + 1 - core
    is_root = p == 0
    outer = (core == 1) & (chip > 0)

    def wrapped(index, size):
        return jnp.where(index >= size, index - size, jnp.where(index < 0, index + size, index))

    nears = [2 * wrapped(chip + o, CHIPS) + core for o in range(CHIPS)]
    aboves = [wrapped(z + o, NZ) if o < 9 else wrapped(z + o - NZ, NZ) for o in range(NZ)]

    def near(o):
        return nears[o]

    def above(o):
        return aboves[o % NZ]

    x, y = lax.div(chip, 4), lax.rem(chip, 4)
    x_odd, y_odd = lax.rem(x, 2), lax.rem(y, 2)
    across, along = 4 - 8 * x_odd, 1 - 2 * y_odd
    square = [(chip + move, c) for move in (across + along, across, along) for c in (core, 1 - core)]
    square.append((chip, 1 - core))

    def part_of(target):
        return 4 * (target // 8 % 2) + 2 * (target // 2 % 2) + target % 2

    mine_part = 2 * x_odd + y_odd
    relay = pl.ds(pl.multiple_of(core * NB + 64 * mine_part, 64), 64)

    barrier = pltpu.get_barrier_semaphore()

    def greet(device):
        pl.semaphore_signal(barrier, inc=1, device_id=device, device_id_type=MESH)

    pivot_copy = pltpu.make_async_copy(pivots, piv, local_sem.at[2])
    panel_copy = pltpu.make_async_copy(panel, pt.at[z], local_sem.at[0])
    slab_copy = pltpu.make_async_copy(slab, rows, local_sem.at[1])
    lanes_copy = pltpu.make_async_copy(pivot_row, pivot_lanes, local_sem.at[3])
    panel_copy.start()
    slab_copy.start()
    pivot_copy.start()
    lanes_copy.start()

    for o in (10, 9, 11, 6, 14):
        greet((near(o), z))
    for o in range(REACH, 0, -1):
        greet((p, above(o)))
        greet((p, above(-o)))
    for o in (2, 5, 7, 8, 13, 15, 1, 3, 4, 12):
        greet((near(o), z))
    for other, c in square[1::2]:
        greet((2 * other + c, z))
    greet((sibling, z))

    @pl.when(is_root)
    def _():
        for o in range(1, CHIPS):
            greet((2 * o + 1, z))

    @pl.when(outer)
    def _():
        greet((0, z))

    panel_copy.wait()
    for k in range(WIDTH):
        for h in range(2):
            piece[2 * (k % 4) + h, k // 4 : k // 4 + 1, :] = pt[z, k : k + 1, h * HALF : (h + 1) * HALF]
    greeted = 2 * REACH + CHIPS + 3
    pl.semaphore_wait(barrier, greeted + jnp.where(is_root, CHIPS - 1, jnp.where(outer, 1, 0)))

    for o in (REACH, -REACH):
        pl.semaphore_signal(known, inc=1, device_id=(p, above(o)), device_id_type=MESH)

    def remote(src, dst, send, recv, device):
        return pltpu.make_async_remote_copy(
            src_ref=src, dst_ref=dst, send_sem=send, recv_sem=recv, device_id=device, device_id_type=MESH
        )

    def ring_copy(direction, place, piece_of):
        jump = 2 - place % 2
        block = above(-direction * (place - jump))
        d = (direction + 1) // 2
        if place % 2:
            part, arrived = pt.at[block], leaf_recv.at[place // 4]
        else:
            part = pt.at[block, pl.ds(8 * (2 * piece_of // PARTS), 8)]
            if PARTS == 1:
                part = pt.at[block]
            elif PARTS > 2:
                width = 2 * ROWS // PARTS
                part = pt.at[block, pl.ds(8 * (2 * piece_of // PARTS), 8), pl.ds(width * (piece_of % (PARTS // 2)), width)]
            arrived = leaf_recv.at[1] if place == LAST else ring_recv.at[d, place // 2 - 1, piece_of]
        return remote(part, part, ring_send, arrived, (p, above(direction * jump)))

    def ring_pass(place):
        for q in range(PARTS):
            for d in (1, -1):
                if place > 0:
                    ring_copy(d, place, q).wait_recv()
                if place + 2 < LAST or (2 * q < PARTS) == (d == 1):
                    ring_copy(d, place + 2, q).start()
        for leaf in LEAVES_AFTER[place]:
            for d in (1, -1):
                ring_copy(d, leaf, 0).start()

    def ring_leaves(group):
        blocks = pt.at[pl.ds(0, 4 + group)]
        remote(blocks, blocks, ring_send, leaf_recv.at[group], (p, z)).wait_recv()

    ring_all = remote(pt.at[pl.ds(0, NZ - 1)], pt.at[pl.ds(0, NZ - 1)], ring_send, leaf_recv.at[0], (p, z))

    def a_copy(target, part):
        return remote(piece.at[part], piece_in.at[z], a_send, a_recv, (target, z))

    def lead_copy(target, t_chip, t_core):
        src = rows.at[pl.ds(t_chip * 16, 16), pl.ds(t_core * HALF, HALF)]
        return remote(src, lead_in, lead_send, lead_recv, (target, z))

    def rs_copy(o):
        t_chip = wrapped(chip + o, CHIPS)
        return remote(masked.at[2, pl.ds(pl.multiple_of(t_chip * 16, 16), 16)], landed.at[o], rs_send, rs_recv, (near(o), z))

    def ag_copy(o):
        return remote(mine, gathered.at[core, chip], ag_send, ag_recv, (near(o), z))

    def b_copy(o):
        return remote(piece_in.at[z], piece_in.at[z], b_send, b_recv, (p, above(o)))

    sib_p = remote(masked.at[1 - core], from_sibling, p_send, p_recv, (sibling, z))
    sib_g = remote(gathered.at[core], gathered.at[core], g_send, g_recv, (sibling, z))
    c_copies = [remote(wide.at[relay], wide.at[relay], c_send, c_recv, (2 * other + c, z)) for other, c in square]
    here = (p, z)
    rs_all = remote(masked.at[2, pl.ds(0, 15 * 16)], landed.at[pl.ds(1, 15)], rs_send, rs_recv, here)
    ag_all = remote(gathered.at[core, pl.ds(0, 15)], gathered.at[core, pl.ds(0, 15)], ag_send, ag_recv, here)
    c_all = remote(wide.at[pl.ds(0, 448)], wide.at[pl.ds(0, 448)], c_send, c_recv, here)
    b_all = remote(piece_in.at[pl.ds(0, 15)], piece_in.at[pl.ds(0, 15)], b_send, b_recv, here)
    lead_all = remote(rows.at[pl.ds(0, 31 * 8)], rows.at[pl.ds(0, 31 * 8)], lead_send, lead_recv, here)
    a_all = remote(masked.at[0, pl.ds(0, 124)], masked.at[0, pl.ds(0, 124)], a_send, a_recv, here)

    def a_start():
        @pl.when(is_root)
        def _():
            for t in sorted(range(1, 2 * CHIPS), key=lambda t: -(2 - abs(t // 8 - 2) - abs(t // 2 % 4 - 2))):
                a_copy(t, part_of(t)).start()
            piece_in[z] = piece[0]

    def lead_start():
        @pl.when(is_root)
        def _():
            for t in range(1, 2 * CHIPS):
                lead_copy(t, t // 2, t % 2).start()
            lead_in[...] = rows[0:16, 0:HALF]

    def b_start():
        @pl.when(p > 0)
        def _():
            a_copy(0, 0).wait_recv()
        pl.semaphore_wait(known, 2)
        for o in (8, 7, 9, 6, 10, 5, 11, 4, 12, 3, 13, 2, 14, 1, 15):
            b_copy(o).start()

    def c_start():
        b_all.wait_recv()
        for k in range(NZ):
            column[4 * k : 4 * k + 4, :] = piece_in[k]
        wide[relay, :] = column[...]
        for copy in c_copies:
            copy.start()

    def rs_start():
        sib_p.wait_recv()
        masked[2] = masked[core] + from_sibling[...]
        for o in range(1, CHIPS):
            rs_copy(o).start()

    def ag_start():
        rs_all.wait_recv()
        @pl.when(p > 0)
        def _():
            lead_copy(0, 0, 0).wait_recv()
        total = masked[2, pl.ds(chip * 16, 16)]
        for o in range(1, CHIPS):
            total = total + landed[o]
        mine[0] = total
        mine[1] = lead_in[...]
        gathered[core, chip] = mine[...]
        for o in range(1, CHIPS):
            ag_copy(o).start()

    def g_start():
        ag_all.wait_recv()
        sib_g.start()

    def swap_rows():
        for h in range(2):
            leading[:, h * HALF : (h + 1) * HALF] = gathered[h, :, 1].reshape(NB, HALF)
        lead_high, lead_low = split(leading[...])
        ones = jnp.ones((NB, COLS), BF16)
        for n in range(ROWS // CHUNK):
            index = lax.broadcasted_iota(jnp.int32, (CHUNK, NB), 0) + (row_start + n * CHUNK)
            chosen = jnp.where(index == pivot_lanes[...], 1.0, 0.0).astype(BF16)
            replaced = dot1(chosen, lead_high) + dot1(chosen, lead_low)
            part = slice(n * CHUNK, (n + 1) * CHUNK)
            rows[part, :] = jnp.where(dot1(chosen, ones) > 0.5, replaced, rows[part, :])

    def block_rows(place):
        return pl.ds(pl.multiple_of(WIDTH * above(place), WIDTH), WIDTH)

    def split_blocks(*places):
        for place in places:
            high, low = split(pt[above(place)])
            panel_high[block_rows(place), :] = high
            panel_low[block_rows(place), :] = low

    a_start()
    ring_pass(0)
    pivot_copy.wait()
    lanes_copy.wait()
    slab_copy.wait()

    row_start = p * ROWS

    def pick(k, carry):
        local = piv[k] - row_start
        held = (local >= 0) & (local < ROWS)
        row = rows[pl.ds(jnp.clip(local, 0, ROWS - 1), 1), :]
        row = jnp.where(held, row, 0.0)
        masked[0, pl.ds(k, 1), :] = row[:, :HALF]
        masked[1, pl.ds(k, 1), :] = row[:, HALF:]
        return carry

    lax.fori_loop(0, NB, pick, 0, unroll=8)

    sib_p.start()
    lead_start()
    rs_start()
    b_start()
    ring_pass(2)
    split_blocks(0, 2, -2)
    ag_start()
    ring_pass(4)
    split_blocks(4, -4)
    c_start()
    ring_pass(6)
    g_start()
    ring_leaves(0)
    split_blocks(1, -1, 3, -3, 6, -6)
    @pl.when(is_root)
    def _():
        lead_all.wait_send()
    c_all.wait_recv()

    for h in range(2):
        for g in range(4):
            upper_t[pl.ds(h * NB + g, 64, stride=4), :] = wide[h * NB + 64 * g : h * NB + 64 * g + 64, :]
    corner = split(upper_t[NB : NB + HALF, :].T)
    top = split(invert(upper_t[0:HALF, :].T))
    bottom = split(invert(upper_t[NB + HALF : 2 * NB, :].T))

    def pivot_half(h):
        return jnp.concatenate([gathered[c, 8 * h : 8 * h + 8, 0].reshape(HALF, HALF) for c in range(2)], axis=1)

    sib_g.wait_recv()
    upper_first = dot3(top, split(pivot_half(0)))
    upper_second = dot3(bottom, split(pivot_half(1) - dot3(corner, split(upper_first))))
    upper = jnp.concatenate([upper_first, upper_second], axis=0)
    upper_parts = split(upper)
    upper_high[...], upper_low[...] = upper_parts
    swap_rows()

    for place in LATE:
        for ref in (panel_high, panel_low):
            ref[block_rows(place), :] = jnp.zeros((WIDTH, ROWS), BF16)
    for n in range(ROWS // CHUNK):
        part = slice(n * CHUNK, (n + 1) * CHUNK)
        rows[part, :] -= dot3((panel_high[:, part], panel_low[:, part]), upper_parts, 0)

    count = len(LATE) * WIDTH
    late_panel[3 * count :, :] = jnp.zeros((NB - 3 * count, ROWS), BF16)
    late_upper[3 * count :, :] = jnp.zeros((NB - 3 * count, COLS), BF16)
    for i, place in enumerate(LATE):
        for term, ref in enumerate((upper_high, upper_low, upper_high)):
            late_upper[term * count + i * WIDTH : term * count + (i + 1) * WIDTH, :] = ref[block_rows(place), :]

    ring_leaves(1)
    for i, place in enumerate(LATE):
        high, low = split(pt[above(place)])
        for term, value in enumerate((high, high, low)):
            late_panel[term * count + i * WIDTH : term * count + (i + 1) * WIDTH, :] = value

    for n in range(ROWS // CHUNK):
        part = slice(n * CHUNK, (n + 1) * CHUNK)
        value = rows[part, :] - dot1(late_panel[:, part], late_upper[...], 0)
        if n == 0:
            value = jnp.where(is_root, upper, value)
        out[part, :] = value

    for copy in (sib_p, sib_g, rs_all, ag_all, b_all, c_all, ring_all):
        copy.wait_send()
    @pl.when(is_root)
    def _():
        a_all.wait_send()


def split(a):
    high = a.astype(BF16)
    return high, (a - high.astype(F32)).astype(BF16)


def dot1(a, b, dim=1):
    return lax.dot_general(a, b, (((dim,), (0,)), ((), ())), preferred_element_type=F32)


def dot3(a, b, dim=1):
    return dot1(a[0], b[0], dim) + (dot1(a[0], b[1], dim) + dot1(a[1], b[0], dim))


def invert(square):
    row = lax.broadcasted_iota(jnp.int32, (HALF, HALF), 0)
    col = lax.broadcasted_iota(jnp.int32, (HALF, HALF), 1)
    lower = jnp.where(row > col, square, 0.0)
    blocks = HALF // BASE
    on_diag = (row // BASE) == (col // BASE)
    packed = jnp.sum(jnp.where(on_diag, lower, 0.0).reshape(blocks, BASE, HALF), axis=0)
    small_row = lax.broadcasted_iota(jnp.int32, (BASE, HALF), 0)
    small_col = lax.broadcasted_iota(jnp.int32, (BASE, HALF), 1)
    inverse = jnp.where(small_row == small_col % BASE, 1.0, 0.0)
    for k in range(BASE - 1):
        factor = jnp.take_along_axis(packed, (small_col // BASE) * BASE + k, axis=1)
        inverse = inverse - factor * inverse[k : k + 1, :]
    inverse = jnp.where(on_diag, jnp.concatenate([inverse] * blocks, axis=0), 0.0)
    size = BASE
    while size < HALF:
        same = (row // (2 * size)) == (col // (2 * size))
        below = same & ((row // size) % 2 == 1) & ((col // size) % 2 == 0)
        parts = split(inverse)
        inverse = inverse - dot3(parts, split(dot3(split(jnp.where(below, lower, 0.0)), parts)))
        size *= 2
    return inverse


def local(slab, panel, pivots):
    dma = pltpu.SemaphoreType.DMA
    hbm = pl.BlockSpec(memory_space=pltpu.HBM)
    return pl.pallas_call(
        exchange_kernel,
        name="exchange",
        out_shape=jax.ShapeDtypeStruct((ROWS, COLS), F32),
        in_specs=[hbm] * 4,
        out_specs=pl.BlockSpec(memory_space=pltpu.VMEM),
        scratch_shapes=[
            pltpu.VMEM((NZ, WIDTH, ROWS), F32),
            pltpu.VMEM((2, CHIPS, 2, 16, HALF), F32),
            pltpu.VMEM((2 * NB, HALF), F32),
            pltpu.SMEM((NB,), jnp.int32),
            pltpu.VMEM((1, NB), jnp.int32),
            pltpu.VMEM((2 * NB, HALF), F32),
            pltpu.VMEM((NB, COLS), F32),
            pltpu.VMEM((NB, ROWS), BF16),
            pltpu.VMEM((NB, ROWS), BF16),
            pltpu.VMEM((NB, COLS), BF16),
            pltpu.VMEM((NB, COLS), BF16),
            pltpu.VMEM((NB, ROWS), BF16),
            pltpu.VMEM((NB, COLS), BF16),
            pltpu.VMEM((ROWS, COLS), F32),
            pltpu.VMEM((3, NB, HALF), F32),
            pltpu.VMEM((NB, HALF), F32),
            pltpu.VMEM((CHIPS, 16, HALF), F32),
            pltpu.VMEM((2, 16, HALF), F32),
            pltpu.VMEM((16, HALF), F32),
            pltpu.VMEM((8, 4, HALF), F32),
            pltpu.VMEM((NZ, 4, HALF), F32),
            pltpu.VMEM((4 * NZ, HALF), F32),
            dma((4,)),
            dma, dma((2, 3, 4)), dma((2,)),
            dma, dma,
            dma, dma,
            dma, dma,
            dma, dma,
            dma, dma,
            dma, dma,
            dma, dma,
            dma, dma,
            pltpu.SemaphoreType.REGULAR,
        ],
        compiler_params=pltpu.CompilerParams(
            collective_id=0, has_side_effects=True, vmem_limit_bytes=24576 * 1024
        ),
    )(*(pltpu.with_memory_space_constraint(a, pltpu.HBM) for a in (pivots, pivots.reshape(1, NB), slab, panel.T)))


def solution(mesh):
    return jax.shard_map(
        local,
        mesh=mesh,
        in_specs=(P("prow", "pcol"), P("prow", "pcol"), P()),
        out_specs=P("prow", "pcol"),
        check_vma=False,
    )
```
